128 devices in a mesh: ctx: 8 (over z, core), tp: 8 (over y_lo, x), grp: 2 (over y_hi).
Axes of the slice: x: 4, y: 4 (y_hi: 2, y_lo: 2; y = y_hi * 2 + y_lo), z: 4, core: 2. Of those that a mesh axis runs over, the one named last changes fastest.
Arguments:
- merged_hidden: bfloat16 [8192, 5120], P(('ctx', 'grp')), may hold values from -40 to 40
- counts: int32 [16], replicated, may hold values from 1 to 32, 192 in all
- owner: int32 [16, 32], replicated, may hold values from 0 to 15, as said below
- down_proj: bfloat16 [5120, 8192], P(None, 'tp'), may hold values from -0.078125 to 0.078125
- text_embed: bfloat16 [8192, 8192], P(('ctx', 'grp'), 'tp'), may hold values from -64 to 64
- norm_gain: float32 [8192], replicated, may hold values from 0.1 to 1.9
- w_query: bfloat16 [8192, 4096], P(None, 'tp')
- w_key: bfloat16 [8192, 1024], P(None, 'tp')
- w_value: bfloat16 [8192, 1024], P(None, 'tp'), may hold values from -0.0625 to 0.0625
Outputs:
- attended: bfloat16 [8192, 4096], P(('ctx', 'grp'), 'tp')
The draws below stay inside these ranges and needn't reach their ends.
Inputs may be any that keep to these rules, and one draw needn't show every extreme that they name: `owner`: for each encoder device, window slot i goes to shard p[i mod (8 * 2)] for a permutation p of the shards drawn for that device, so one device's live windows reach one shard at most 2 times. `counts`: the live windows of all devices number 192.
All inputs are finite; a program needn't handle non-finite values.
Results may differ from the reference program's by a relative error of at most 0.013.
The reference program's roundings to bfloat16 on the way (of `image`, `sequence` and `normed`) count: a program that leaves them out, or rounds other values in their place, can miss the bound.
Values may be sent and summed in bfloat16 or wider, within the bound.
A program may use at most 256 MiB of HBM per device.

```python
import math
import jax
import jax.numpy as jnp
import numpy as np
from jax import lax

D = 8192
KVH = 8
HD = 128
HQ = 32
HID = 5120
WIN = 16
SEQ_DEV = 512
WCAP = 32
WTOT = 192
SEQ = 8192
N_CTX = 8
N_GRP = 2


def draw_merged_hidden(key, part):
    key = jax.random.fold_in(key, 3)
    first = jax.random.fold_in(key, 0)
    base = jnp.clip(jax.random.normal(first, (SEQ, HID), jnp.float32), -4.0, 4.0)
    return base.astype(jnp.bfloat16)


def draw_owner(key, part):
    key = jax.random.fold_in(key, 5)
    shards = N_CTX * N_GRP
    scores = jax.random.randint(key, (shards, shards), 0, 1 << 20) * shards + jnp.arange(shards, dtype=jnp.int32)[None, :]
    order = jnp.argsort(scores, axis=1, stable=True).astype(jnp.int32)
    return jnp.tile(order, (1, WCAP // shards))


def draw_text_embed(key, part):
    key = jax.random.fold_in(key, 7)
    first = jax.random.fold_in(key, 0)
    base = jnp.clip(jax.random.normal(first, (SEQ, D), jnp.float32), -4.0, 4.0)
    return base.astype(jnp.bfloat16)


def draw_w_query(key, part):
    key = jax.random.fold_in(key, 11)
    base = jnp.clip(jax.random.normal(key, (D, HQ * HD), jnp.float32), -6.0, 6.0) * D ** (-0.5)
    return base.astype(jnp.bfloat16)


def draw_w_key(key, part):
    key = jax.random.fold_in(key, 13)
    base = jnp.clip(jax.random.normal(key, (D, KVH * HD), jnp.float32), -6.0, 6.0) * D ** (-0.5)
    return base.astype(jnp.bfloat16)


def steps_of(key, shape, cuts, low, high):
    level = 1.0
    for axis_at, blocks in cuts:
        draws = jax.random.uniform(jax.random.fold_in(jax.random.fold_in(key, 6), axis_at), (blocks,), jnp.float32, low / len(cuts), high / len(cuts))
        level = level * jnp.repeat(jnp.exp(draws), shape[axis_at] // blocks).reshape((-1,) + (1,) * (len(shape) - 1 - axis_at))
    return level


def profile(amount, total, most, skew):
    loads = [(1 << 20) // math.isqrt(grade ** skew) + 1 for grade in range(2, amount + 1)]
    rest, given = total - most - (amount - 1), [1] * (amount - 1)
    while rest > 0:
        movable = [i for i in range(amount - 1) if given[i] < most]
        pool, budget = sum([loads[i] for i in movable]), rest
        for i in movable:
            more = min(most - given[i], max(1, budget * loads[i] // pool), rest)
            given[i] = given[i] + more
            rest = rest - more
    return np.array([most] + given)


def uneven_parts(key, number_of, total, reach, slope):
    if number_of == 2:
        one = jax.random.randint(key, (), max(1, total - reach), min(reach, total - 1) + 1)
        return jnp.stack([one, total - one])
    sizes = jnp.asarray(profile(number_of, total, reach, slope), jnp.int32)
    couples = (number_of - 1) // 2
    donor, receiver = sizes[1:1 + 2 * couples:2], sizes[2:2 + 2 * couples:2]
    margin = jnp.minimum(donor - 1, reach - receiver)
    passed = jax.random.randint(jax.random.fold_in(key, 1), (couples,), 0, 1 << 20) % (margin + 1)
    sizes = sizes.at[1:1 + 2 * couples:2].set(donor - passed).at[2:2 + 2 * couples:2].set(receiver + passed)
    return sizes[jax.random.permutation(jax.random.fold_in(key, 2), number_of)]


def centred(own_key, extent, spread, limit, pieces=(), kind=jnp.bfloat16):
    entries = spread * jax.random.normal(own_key, extent, jnp.float32)
    if pieces:
        entries = entries * steps_of(own_key, extent, pieces, -0.22, 0.18)
    return jnp.clip(entries, -limit, limit).astype(kind)


def setup_inputs(seed: int = 0) -> dict:
    arg_keys = jax.random.split(jax.random.key(seed), 10)
    return {
        "merged_hidden": draw_merged_hidden(jax.random.fold_in(arg_keys[9], 71), 0),
        "counts": uneven_parts(arg_keys[1], N_CTX * N_GRP, WTOT, WCAP, 2).astype(jnp.int32),
        "owner": draw_owner(jax.random.fold_in(arg_keys[9], 71), 0),
        "down_proj": centred(arg_keys[3], (HID, D), HID ** -0.5, 0.078125, ((1, 8),)),
        "text_embed": draw_text_embed(jax.random.fold_in(arg_keys[9], 71), 0),
        "norm_gain": jnp.clip(1.0 + 0.18 * jax.random.normal(arg_keys[5], (D,), jnp.float32), 0.1, 1.9),
        "w_query": draw_w_query(jax.random.fold_in(arg_keys[9], 71), 0),
        "w_key": draw_w_key(jax.random.fold_in(arg_keys[9], 71), 0),
        "w_value": centred(arg_keys[8], (D, KVH * HD), D ** -0.5, 0.0625, ((1, 8),)),
    }


def reference(merged_hidden, counts, owner, down_proj, text_embed, norm_gain, w_query, w_key, w_value):
    holders = N_CTX * N_GRP
    wins_dev = SEQ_DEV // WIN
    slot_ids = jnp.arange(WCAP, dtype=jnp.int32)
    live = slot_ids[None, :] < counts[:, None]
    shards = jnp.arange(holders, dtype=jnp.int32)
    hits = ((owner[:, :, None] == shards[None, None, :]) & live[:, :, None]).astype(jnp.int32)
    per_pair = lax.optimization_barrier(jnp.sum(hits, axis=1, dtype=jnp.int32))
    before = jnp.cumsum(per_pair, axis=0, dtype=jnp.int32) - per_pair
    earlier = jnp.cumsum(hits, axis=1, dtype=jnp.int32) - hits
    rank_own = lax.optimization_barrier(jnp.sum(earlier * hits, axis=2, dtype=jnp.int32))
    before_own = lax.optimization_barrier(jnp.sum(before[:, None, :] * hits, axis=2, dtype=jnp.int32))
    target = (owner * wins_dev + before_own + rank_own).astype(jnp.int32)
    chosen = jnp.nonzero(live.reshape(-1), size=WTOT)[0].astype(jnp.int32)
    windows = merged_hidden.reshape(holders * WCAP, WIN, HID)[chosen].reshape(WTOT * WIN, HID)
    image = jnp.dot(windows, down_proj, preferred_element_type=jnp.float32).astype(jnp.bfloat16)
    places = target.reshape(-1)[chosen].astype(jnp.int32)
    grid = text_embed.reshape(SEQ // WIN, WIN, D)
    sequence = grid.at[places].set(image.reshape(WTOT, WIN, D)).reshape(SEQ, D)
    values32 = sequence.astype(jnp.float32)
    scale = lax.rsqrt(lax.optimization_barrier(jnp.mean(values32 * values32, axis=1, keepdims=True)) + 1e-06)
    normed = (values32 * scale * norm_gain[None, :]).astype(jnp.bfloat16)
    queries = jnp.dot(normed, w_query, preferred_element_type=jnp.float32).astype(jnp.bfloat16)
    keys = jnp.dot(normed, w_key, preferred_element_type=jnp.float32).astype(jnp.bfloat16)
    values = jnp.dot(normed, w_value, preferred_element_type=jnp.float32).astype(jnp.bfloat16)
    group = HQ // KVH
    q_heads = queries.reshape(SEQ, HQ, HD).transpose(1, 0, 2)
    k_heads = keys.reshape(SEQ, KVH, HD).transpose(1, 0, 2)
    v_heads = values.reshape(SEQ, KVH, HD).transpose(1, 0, 2)
    positions = jnp.arange(SEQ, dtype=jnp.int32)
    causal = positions[:, None] >= positions[None, :]

    def one_head(head):
        query = q_heads[head]
        key_head = k_heads[head // group]
        value_head = v_heads[head // group]
        scores = jnp.dot(query, key_head.T, preferred_element_type=jnp.float32) * HD ** (-0.5)
        scores = jnp.where(causal, scores, -jnp.inf)
        probs = jax.nn.softmax(scores, axis=1).astype(jnp.bfloat16)
        return jnp.dot(probs, value_head, preferred_element_type=jnp.float32).astype(jnp.bfloat16)
    result = lax.map(one_head, jnp.arange(HQ, dtype=jnp.int32))
    return result.transpose(1, 0, 2).reshape(SEQ, HQ * HD)
```

```python
import functools
import math

import jax
import jax.numpy as jnp
from jax import lax
from jax.experimental import pallas as pl
from jax.experimental.pallas import tpu as pltpu
from jax.sharding import PartitionSpec as P

HD = 128
NC = 4
MESH = pl.DeviceIdType.MESH
NEG = float("-inf")


def route_tables(counts, owner, holders, wcap):
    slot_ids = jnp.arange(wcap, dtype=jnp.int32)
    live = slot_ids[None, :] < counts[:, None]
    shards = jnp.arange(holders, dtype=jnp.int32)
    hits = ((owner[:, :, None] == shards[None, None, :]) & live[:, :, None]).astype(jnp.int32)
    per_pair = jnp.sum(hits, axis=1, dtype=jnp.int32)
    before = jnp.cumsum(per_pair, axis=0, dtype=jnp.int32) - per_pair
    earlier = jnp.cumsum(hits, axis=1, dtype=jnp.int32) - hits
    rank = jnp.sum(earlier * hits, axis=2, dtype=jnp.int32)
    return (live, per_pair, before, rank)


def layer_kernel(
    own_in, gain, wq_in, wk_in, wv_in, out,
    seq, wq, wkv, q, kv, m, l, acc, acc_q, acc_kv,
    ld_sem, w_sem, gs, gr, ks, kr, fs, fr,
):
    rows, cols = own_in.shape
    chunk = rows // NC
    half = chunk // 2
    heads = q.shape[0]
    ctx = lax.axis_index("ctx")
    tp = lax.axis_index("tp")
    yh = lax.axis_index("grp")
    z, core = lax.div(ctx, 2), lax.rem(ctx, 2)
    yl, x = lax.div(tp, 4), lax.rem(tp, 4)
    rank = ctx * 2 + yh

    def at(dx, dy):
        return lax.rem(yl + dy, 2) * 4 + lax.rem(x + dx, 4)

    to_xp, to_xm, to_yp = {"tp": at(1, 0)}, {"tp": at(3, 0)}, {"tp": at(0, 1)}
    sibling = {"ctx": z * 2 + 1 - core}

    def mate(dz, dy):
        return {
            "ctx": lax.rem(z + dz, 4) * 2 + core,
            "grp": lax.rem(yh + dy, 2),
        }

    own_load = []
    for i in range(NC):
        r = pl.ds(i * chunk, chunk)
        own_load.append(
            pltpu.make_async_copy(own_in.at[r], seq.at[0, r], ld_sem.at[i])
        )
        own_load[i].start()
    w_load = [
        pltpu.make_async_copy(wk_in, wkv.at[:, :, pl.ds(0, HD)], w_sem.at[0]),
        pltpu.make_async_copy(wv_in, wkv.at[:, :, pl.ds(HD, HD)], w_sem.at[1]),
        pltpu.make_async_copy(wq_in, wq, w_sem.at[2]),
    ]
    for c in w_load:
        c.start()

    barrier = pltpu.get_barrier_semaphore()
    partners = [to_xp, to_xm, to_yp, sibling]
    for n in range(1, 8):
        partners.append(mate(n // 2, n % 2))
    for dev in partners:
        pl.semaphore_signal(barrier, inc=1, device_id=dev, device_id_type=MESH)
    pl.semaphore_wait(barrier, len(partners))

    def remote(src, dst, ssem, rsem, dev):
        return pltpu.make_async_remote_copy(
            src_ref=src, dst_ref=dst, send_sem=ssem, recv_sem=rsem,
            device_id=dev, device_id_type=MESH,
        )

    moves = {}

    def send(i, name, src_slot, dst_slot, r, dev, index):
        c = remote(
            seq.at[src_slot, r], seq.at[dst_slot, r], gs.at[i, index], gr.at[i, index], dev
        )
        c.start()
        moves[i, name] = c

    def whole(i):
        return pl.ds(i * chunk, chunk)

    def first(i):
        own_load[i].wait()
        send(i, "own_y", 0, 3, whole(i), to_yp, 0)
        send(i, "own_xp", 0, 1, whole(i), to_xp, 1)
        send(i, "own_xm", 0, 2, whole(i), to_xm, 2)

    def second(i):
        moves[i, "own_xp"].wait_recv()
        send(i, "opp_a", 1, 6, pl.ds(i * chunk, half), to_xp, 3)
        moves[i, "own_xm"].wait_recv()
        send(i, "opp_b", 2, 6, pl.ds(i * chunk + half, half), to_xm, 4)
        moves[i, "own_y"].wait_recv()
        send(i, "mate_xp", 3, 4, whole(i), to_xp, 5)
        send(i, "mate_xm", 3, 5, whole(i), to_xm, 6)

    def third(i):
        moves[i, "opp_a"].wait_recv()
        moves[i, "opp_b"].wait_recv()
        send(i, "opp_y", 6, 7, whole(i), to_yp, 7)

    places = [(0, 0), (3, 0), (1, 0), (0, 1), (3, 1), (1, 1), (2, 0), (2, 1)]
    kv_moves = {}

    def project(i):
        r = whole(i)
        for name in ("mate_xp", "mate_xm", "opp_y"):
            moves[i, name].wait_recv()
        total = jnp.zeros((chunk, 1), jnp.float32)
        for k in range(8):
            v = seq[k, r].astype(jnp.float32)
            total = total + jnp.sum(v * v, axis=1, keepdims=True)
        scale = lax.rsqrt(total / (8 * cols) + 1e-06)
        for k in range(8):
            b = at(*places[k])
            v = seq[k, r].astype(jnp.float32)
            normed = (v * scale * gain[pl.ds(b, 1), :]).astype(jnp.bfloat16)
            part_kv = jnp.dot(normed, wkv[b], preferred_element_type=jnp.float32)
            part_q = jnp.dot(normed, wq[b], preferred_element_type=jnp.float32)
            if k == 0:
                acc_kv[...] = part_kv
                acc_q[...] = part_q
            else:
                acc_kv[...] += part_kv
                acc_q[...] += part_q
        kv[0, 0, r] = acc_kv[...].astype(jnp.bfloat16)
        for h in range(heads):
            q[h, r] = acc_q[:, h * HD:(h + 1) * HD].astype(jnp.bfloat16)
        for n in range(1, 8):
            c = remote(
                kv.at[0, 0, r], kv.at[n, 0, r], ks.at[n, i], kr.at[n, i], mate(n // 2, n % 2)
            )
            kv_moves[n, i] = c
            if n == 1:
                c.start()
            else:
                @pl.when(z + n // 2 <= 3)
                def _():
                    c.start()

    first(0)
    first(1)
    for c in w_load:
        c.wait()
    for i in range(NC + 2):
        if i < NC:
            second(i)
        if i + 2 < NC:
            first(i + 2)
        if 0 <= i - 1 < NC:
            third(i - 1)
        if 0 <= i - 2 < NC:
            project(i - 2)

    m[...] = jnp.full(m.shape, NEG, jnp.float32)
    l[...] = jnp.zeros(l.shape, jnp.float32)
    acc[...] = jnp.zeros(acc.shape, jnp.float32)
    scale2 = math.log2(math.e) / math.sqrt(HD)

    def attend(n, c, masked):
        tile = min(256, rows)
        for h in range(heads):
            for t in range(rows // tile):
                r = pl.ds(t * tile, tile)
                s = lax.dot_general(
                    q[h, r], kv[n, c, :, :HD], (((1,), (1,)), ((), ())),
                    preferred_element_type=jnp.float32,
                )
                if masked:
                    qi = lax.broadcasted_iota(jnp.int32, s.shape, 0) + t * tile
                    ki = lax.broadcasted_iota(jnp.int32, s.shape, 1)
                    s = jnp.where(ki <= qi, s, NEG)
                old = m[h, r]
                new = jnp.maximum(old, jnp.max(s, axis=1, keepdims=True))
                m[h, r] = new
                fade = jnp.exp2((old - new) * scale2)
                p = jnp.exp2((s - new[:, :1]) * scale2)
                part = p[:, :128]
                for j in range(1, rows // 128):
                    part = part + p[:, j * 128:(j + 1) * 128]
                l[h, r] = l[h, r] * fade + part
                acc[h, r] = acc[h, r] * fade + jnp.dot(
                    p.astype(jnp.bfloat16), kv[n, c, :, HD:],
                    preferred_element_type=jnp.float32,
                )

    def forward(n):
        return remote(kv.at[n, 0], kv.at[n, 1], fs.at[n], fr.at[n], sibling)

    forward(0).start()
    attend(0, 0, True)

    @pl.loop(1, 8)
    def _(n):
        dz, dy = lax.div(n, 2), lax.rem(n, 2)

        @pl.when(z - dz >= 0)
        def _():
            for i in range(NC):
                r = whole(i)
                remote(
                    kv.at[0, 0, r], kv.at[n, 0, r], ks.at[n, i], kr.at[n, i], sibling
                ).wait_recv()
            forward(n).start()

        src = (z - dz) * 4 + core * 2 + lax.rem(yh + dy, 2)

        @pl.when(jnp.logical_and(z - dz >= 0, src < rank))
        def _():
            attend(n, 0, False)

    @pl.loop(0, 8)
    def _(n):
        dz, dy = lax.div(n, 2), lax.rem(n, 2)

        @pl.when(z - dz >= 0)
        def _():
            forward(n).wait_recv()

        src = (z - dz) * 4 + (1 - core) * 2 + lax.rem(yh + dy, 2)

        @pl.when(jnp.logical_and(z - dz >= 0, src < rank))
        def _():
            attend(n, 1, False)

    for h in range(heads):
        total = jnp.sum(l[h], axis=1, keepdims=True)
        out[:, h * HD:(h + 1) * HD] = (acc[h] / total).astype(jnp.bfloat16)

    for c in moves.values():
        c.wait_send()
    for (n, i), c in kv_moves.items():
        if n == 1:
            c.wait_send()
        else:
            @pl.when(z + n // 2 <= 3)
            def _():
                c.wait_send()

    @pl.loop(0, 8)
    def _(n):
        @pl.when(z - lax.div(n, 2) >= 0)
        def _():
            forward(n).wait_send()


def layer(own_cols, norm_gain, w_query, w_key, w_value):
    rows, cols = own_cols.shape
    blocks = norm_gain.shape[0] // cols
    q_cols = w_query.shape[1]
    heads = q_cols // HD
    any_space = pl.BlockSpec(memory_space=pl.ANY)
    vmem = pl.BlockSpec(memory_space=pltpu.VMEM)
    dma = pltpu.SemaphoreType.DMA
    return pl.pallas_call(
        layer_kernel,
        out_shape=jax.ShapeDtypeStruct((rows, q_cols), jnp.bfloat16),
        in_specs=[any_space, vmem, any_space, any_space, any_space],
        out_specs=vmem,
        scratch_shapes=[
            pltpu.VMEM((8, rows, cols), jnp.bfloat16),
            pltpu.VMEM((blocks, cols, q_cols), jnp.bfloat16),
            pltpu.VMEM((blocks, cols, 2 * HD), jnp.bfloat16),
            pltpu.VMEM((heads, rows, HD), jnp.bfloat16),
            pltpu.VMEM((8, 2, rows, 2 * HD), jnp.bfloat16),
            pltpu.VMEM((heads, rows, 128), jnp.float32),
            pltpu.VMEM((heads, rows, 128), jnp.float32),
            pltpu.VMEM((heads, rows, HD), jnp.float32),
            pltpu.VMEM((rows // NC, q_cols), jnp.float32),
            pltpu.VMEM((rows // NC, 2 * HD), jnp.float32),
            dma((NC,)),
            dma((3,)),
            dma((NC, 8)),
            dma((NC, 8)),
            dma((8, NC)),
            dma((8, NC)),
            dma((8,)),
            dma((8,)),
        ],
        compiler_params=pltpu.CompilerParams(
            collective_id=0, has_side_effects=True, vmem_limit_bytes=60 * 1024 * 1024
        ),
        name="layer",
    )(
        own_cols,
        norm_gain.reshape(blocks, cols),
        w_query.reshape(blocks, cols, q_cols),
        w_key.reshape(blocks, cols, HD),
        w_value.reshape(blocks, cols, HD),
    )


def local(merged_hidden, counts, owner, down_proj, text_embed, norm_gain, w_query, w_key, w_value):
    holders = lax.axis_size(("ctx", "grp"))
    device = lax.axis_index(("ctx", "grp"))
    wcap = owner.shape[1]
    rows_dev = text_embed.shape[0]
    window = rows_dev // wcap
    most = wcap // holders
    windows_dev = rows_dev // window
    live, per_pair, before, rank = route_tables(counts, owner, holders, wcap)
    image = jnp.dot(merged_hidden, down_proj, preferred_element_type=jnp.float32).astype(
        jnp.bfloat16
    )
    my_live = lax.dynamic_index_in_dim(live, device, 0, False)
    my_owner = lax.dynamic_index_in_dim(owner, device, 0, False)
    my_rank = lax.dynamic_index_in_dim(rank, device, 0, False)
    slot_of = my_owner * most + my_rank
    slot_ids = jnp.arange(holders * most, dtype=jnp.int32)
    select = ((slot_of[None, :] == slot_ids[:, None]) & my_live[None, :]).astype(jnp.bfloat16)
    arrivals = lax.dynamic_index_in_dim(per_pair, device, 1, False)
    offsets = lax.dynamic_index_in_dim(before, device, 1, False)
    slot_rank = jnp.arange(most, dtype=jnp.int32)
    dest = (offsets[:, None] + slot_rank[None, :]).reshape(-1)
    valid = (slot_rank[None, :] < arrivals[:, None]).reshape(-1)
    window_ids = jnp.arange(windows_dev, dtype=jnp.int32)
    place = ((dest[None, :] == window_ids[:, None]) & valid[None, :]).astype(jnp.bfloat16)
    filled = jnp.sum(arrivals)
    image_mask = jnp.arange(rows_dev, dtype=jnp.int32) // window < filled
    width = image.shape[1]
    grid = image.reshape(wcap, window, width)
    packed = jnp.einsum("aw,wtc->atc", select, grid, preferred_element_type=jnp.float32).astype(
        jnp.bfloat16
    )
    arrived = lax.all_to_all(
        packed.reshape(holders, most * window, width),
        ("ctx", "grp"),
        split_axis=0,
        concat_axis=0,
        tiled=True,
    )
    width = arrived.shape[-1]
    grid = arrived.reshape(holders * most, window, width)
    placed = jnp.einsum("pa,atc->ptc", place, grid, preferred_element_type=jnp.float32).astype(
        jnp.bfloat16
    )
    own_cols = jnp.where(image_mask[:, None], placed.reshape(rows_dev, width), text_embed)
    return layer(own_cols, norm_gain, w_query, w_key, w_value)


def solution(mesh):
    in_specs = (
        P(("ctx", "grp"), None),
        P(),
        P(),
        P(None, "tp"),
        P(("ctx", "grp"), "tp"),
        P(),
        P(None, "tp"),
        P(None, "tp"),
        P(None, "tp"),
    )
    out_specs = P(("ctx", "grp"), "tp")
    return jax.shard_map(local, mesh=mesh, in_specs=in_specs, out_specs=out_specs, check_vma=False)
```

```python
import functools
import math

import jax
import jax.numpy as jnp
from jax import lax
from jax.experimental import pallas as pl
from jax.experimental.pallas import tpu as pltpu
from jax.sharding import PartitionSpec as P

HD = 128
NC = 4
NJ = 4
AHEAD = 3
MESH = pl.DeviceIdType.MESH
NEG = float("-inf")


def layer_kernel(
    merged_in, down_in, text_in, counts_in, owner_in, gain, wq_in, wk_in, wv_in, out,
    merged, down, packed, arrived, seq, wq, wkv, q, kv, m, l, acc, acc_q, acc_kv,
    in_sem, w_sem, as_sem, ar_sem, gs, gr, ks, kr, fs, fr,
):
    rows, cols = text_in.shape
    shards, wcap = owner_in.shape
    window = rows // wcap
    most = wcap // shards
    part = cols // NJ
    pair_rows = most * window
    chunk = rows // NC
    half = chunk // 2
    heads = q.shape[1]
    ctx = lax.axis_index("ctx")
    tp = lax.axis_index("tp")
    yh = lax.axis_index("grp")
    z, core = lax.div(ctx, 2), lax.rem(ctx, 2)
    yl, x = lax.div(tp, 4), lax.rem(tp, 4)
    rank = ctx * 2 + yh

    def at(dx, dy):
        return lax.rem(yl + dy, 2) * 4 + lax.rem(x + dx, 4)

    to_xp, to_xm, to_yp = {"tp": at(1, 0)}, {"tp": at(3, 0)}, {"tp": at(0, 1)}
    sibling = {"ctx": z * 2 + 1 - core}

    def shard_at(step):
        d = lax.rem(rank + step, shards)
        return d, {"ctx": lax.div(d, 2), "grp": lax.rem(d, 2)}

    barrier = pltpu.get_barrier_semaphore()
    partners = [to_xp, to_xm, to_yp] + [shard_at(n)[1] for n in range(1, shards)]
    for dev in partners:
        pl.semaphore_signal(barrier, inc=1, device_id=dev, device_id_type=MESH)

    def col(j):
        return pl.ds(j * part, part)

    load_merged = pltpu.make_async_copy(merged_in, merged, in_sem.at[0])
    load_text = pltpu.make_async_copy(text_in, seq.at[0], in_sem.at[1])
    load_down = [
        pltpu.make_async_copy(down_in.at[:, col(j)], down.at[j], in_sem.at[2 + j])
        for j in range(NJ)
    ]
    load_w = [
        pltpu.make_async_copy(wk_in, wkv.at[:, :, pl.ds(0, HD)], w_sem.at[0]),
        pltpu.make_async_copy(wv_in, wkv.at[:, :, pl.ds(HD, HD)], w_sem.at[1]),
        pltpu.make_async_copy(wq_in, wq, w_sem.at[2]),
    ]
    load_merged.start()
    for c in load_down:
        c.start()

    def remote(src, dst, ssem, rsem, dev):
        return pltpu.make_async_remote_copy(
            src_ref=src, dst_ref=dst, send_sem=ssem, recv_sem=rsem,
            device_id=dev, device_id_type=MESH,
        )

    def iota(shape, axis):
        return lax.broadcasted_iota(jnp.int32, shape, axis)

    shard_ids = iota((shards, wcap), 0)
    counts_col = jnp.sum(
        jnp.where(iota((shards, shards), 0) == iota((shards, shards), 1), counts_in[...], 0),
        axis=1, keepdims=True,
    )
    live = iota((shards, wcap), 1) < counts_col
    owner = owner_in[...]
    lane_win = lax.div(iota((wcap, rows), 1), window)
    spread = (lane_win == iota((wcap, rows), 0)).astype(jnp.float32)
    my_owner = jnp.sum(
        jnp.where(live & (shard_ids == rank), owner + 1, 0), axis=0, keepdims=True
    ).astype(jnp.float32)
    my_owner = jnp.broadcast_to(my_owner, (8, wcap))
    lane_owner = jnp.dot(my_owner, spread, preferred_element_type=jnp.float32)[:1].astype(jnp.int32)
    lane = iota((1, rows), 1)
    lane_slot = lax.div(lane, window * shards)
    slot_row = jnp.where(
        lane_owner > 0,
        (lane_owner - 1) * pair_rows + lane_slot * window + lax.rem(lane, window),
        -1,
    )
    arrivals = jnp.sum(
        (live & (owner == rank)).astype(jnp.int32), axis=1, keepdims=True
    )
    from_shard = lax.div(iota((shards, rows), 1), pair_rows)
    by_shard = iota((shards, rows), 0)
    before = jnp.sum(jnp.where(by_shard < from_shard, arrivals, 0), axis=0, keepdims=True)
    here = jnp.sum(jnp.where(by_shard == from_shard, arrivals, 0), axis=0, keepdims=True)
    pair_slot = lax.div(lax.rem(lane, pair_rows), window)
    dest_row = jnp.where(
        pair_slot < here, (before + pair_slot) * window + lax.rem(lane, window), -1
    )
    filled = jnp.sum(arrivals, axis=0, keepdims=True) * window
    row_ids = iota((rows, rows), 0)
    select = (row_ids == slot_row).astype(jnp.float32).astype(jnp.bfloat16)
    place = (row_ids == dest_row).astype(jnp.float32).astype(jnp.bfloat16)
    is_image = iota((rows, part), 0) < filled

    def project_image(j):
        load_down[j].wait()
        image = jnp.dot(
            merged[...], down[j], preferred_element_type=jnp.float32
        ).astype(jnp.bfloat16)
        packed[j] = jnp.dot(select, image, preferred_element_type=jnp.float32).astype(
            jnp.bfloat16
        )

    def own_pair():
        return pl.ds(pl.multiple_of(rank * pair_rows, pair_rows), pair_rows)

    a_moves = {}

    def send_windows(j):
        for n in range(1, shards):
            d, dev = shard_at(n)
            there = pl.ds(pl.multiple_of(d * pair_rows, pair_rows), pair_rows)
            c = remote(
                packed.at[j, there], arrived.at[j, own_pair()], as_sem.at[j, n], ar_sem.at[j], dev
            )
            c.start()
            a_moves[j, n] = c
        arrived[j, own_pair(), :] = packed[j, own_pair(), :]

    def place_windows(j):
        others = pl.ds(0, (shards - 1) * pair_rows)
        remote(
            packed.at[j, others], arrived.at[j, others], as_sem.at[j, 0], ar_sem.at[j], sibling
        ).wait_recv()
        placed = jnp.dot(place, arrived[j], preferred_element_type=jnp.float32)
        text = seq[0, :, col(j)]
        seq[0, :, col(j)] = jnp.where(
            is_image, placed, text.astype(jnp.float32)
        ).astype(jnp.bfloat16)

    moves = {}
    units = [(i, j) for i in range(NC) for j in range(NJ)]

    def send(u, name, src_slot, dst_slot, start, size, dev, index):
        i, j = units[u]
        r = pl.ds(i * chunk + start, size)
        c = remote(
            seq.at[src_slot, r, col(j)], seq.at[dst_slot, r, col(j)],
            gs.at[u, index], gr.at[u, index], dev,
        )
        c.start()
        moves[u, name] = c

    def first(u):
        send(u, "own_y", 0, 3, 0, chunk, to_yp, 0)
        send(u, "own_xp", 0, 1, 0, chunk, to_xp, 1)
        send(u, "own_xm", 0, 2, 0, chunk, to_xm, 2)

    def second(u):
        moves[u, "own_xp"].wait_recv()
        send(u, "opp_a", 1, 6, 0, half, to_xp, 3)
        moves[u, "own_xm"].wait_recv()
        send(u, "opp_b", 2, 6, half, half, to_xm, 4)
        moves[u, "own_y"].wait_recv()
        send(u, "mate_xp", 3, 4, 0, chunk, to_xp, 5)
        send(u, "mate_xm", 3, 5, 0, chunk, to_xm, 6)

    def third(u):
        moves[u, "opp_a"].wait_recv()
        moves[u, "opp_b"].wait_recv()
        send(u, "opp_y", 6, 7, 0, chunk, to_yp, 7)

    places = [(0, 0), (3, 0), (1, 0), (0, 1), (3, 1), (1, 1), (2, 0), (2, 1)]
    kv_moves = []

    def project(i):
        r = pl.ds(i * chunk, chunk)
        for u in range(i * NJ, (i + 1) * NJ):
            for name in ("mate_xp", "mate_xm", "opp_y"):
                moves[u, name].wait_recv()
        total = jnp.zeros((chunk, 1), jnp.float32)
        for k in range(8):
            v = seq[k, r].astype(jnp.float32)
            total = total + jnp.sum(v * v, axis=1, keepdims=True)
        scale = lax.rsqrt(total / (8 * cols) + 1e-06)
        for k in range(8):
            b = at(*places[k])
            v = seq[k, r].astype(jnp.float32)
            g = gain[:, pl.ds(pl.multiple_of(b * cols, cols), cols)]
            normed = (v * scale * g).astype(jnp.bfloat16)
            part_kv = jnp.dot(normed, wkv[b], preferred_element_type=jnp.float32)
            part_q = jnp.dot(normed, wq[b], preferred_element_type=jnp.float32)
            if k == 0:
                acc_kv[...] = part_kv
                acc_q[...] = part_q
            else:
                acc_kv[...] += part_kv
                acc_q[...] += part_q
        kv[i, 0, :chunk] = acc_kv[...].astype(jnp.bfloat16)
        own = pl.ds(0, chunk)
        c = remote(
            kv.at[i, 0, own], kv.at[i, 0, pl.ds(chunk, chunk)], ks.at[i, 0], kr.at[i, 0],
            {"grp": 1 - yh},
        )
        c.start()
        kv_moves.append((c, 0))
        onward(i, 0)
        for h in range(heads):
            q[i, h] = acc_q[:, h * HD:(h + 1) * HD].astype(jnp.bfloat16)

    def onward(i, dy):
        r = pl.ds(dy * chunk, chunk)
        for dz in range(1, 4):
            c = remote(
                kv.at[i, 0, r], kv.at[i, dz, r], ks.at[i, 4 * dy + dz], kr.at[i, 4 * dy + dz],
                {"ctx": lax.rem(z + dz, 4) * 2 + core},
            )
            kv_moves.append((c, dz))

            @pl.when(z + dz <= 3)
            def _():
                c.start()

    def share(i, dz):
        return remote(
            kv.at[i, dz, pl.ds(0, 2 * chunk)], kv.at[i, dz, pl.ds(2 * chunk, 2 * chunk)],
            fs.at[i, dz], fr.at[i, dz], sibling,
        )

    def kv_arrive(i, index, dz, dy):
        r = pl.ds(dy * chunk, chunk)
        remote(
            kv.at[i, 0, r], kv.at[i, dz, r], ks.at[i, index], kr.at[i, index], sibling
        ).wait_recv()

    def kv_one(i):
        kv_arrive(i, 0, 0, 1)
        onward(i, 1)
        share(i, 0).start()

    def kv_two(i):
        for dz in range(1, 4):
            @pl.when(z >= dz)
            def _():
                kv_arrive(i, dz, dz, 0)
                kv_arrive(i, 4 + dz, dz, 1)
                share(i, dz).start()

    def kv_three(i):
        share(i, 0).wait_recv()
        for dz in range(1, 4):
            @pl.when(z >= dz)
            def _():
                share(i, dz).wait_recv()

    scale2 = math.log2(math.e) / math.sqrt(HD)

    def attend_block(work, dz, masked):
        def score(n):
            a, h, b = work[n]
            return lax.dot_general(
                q[a, h], kv[b, dz, :, :HD], (((1,), (1,)), ((), ())),
                preferred_element_type=jnp.float32,
            )

        def finish(a, h, b, fade, probs):
            acc[a, h] = acc[a, h] * fade + jnp.dot(
                probs, kv[b, dz, :, HD:], preferred_element_type=jnp.float32
            )

        ahead = score(0)
        pending = None
        for n, (a, h, b) in enumerate(work):
            s = ahead
            if n + 1 < len(work):
                ahead = score(n + 1)
            if masked:
                key = iota(s.shape, 1)
                dc, dy = lax.div(key, 2 * chunk), lax.rem(lax.div(key, chunk), 2)
                peer = jnp.where(dc == 0, core, 1 - core) * 2 + jnp.where(dy == 0, yh, 1 - yh)
                key_pos = peer * rows + b * chunk + lax.rem(key, chunk)
                query_pos = (core * 2 + yh) * rows + a * chunk + iota(s.shape, 0)
                s = jnp.where(key_pos <= query_pos, s, NEG)
            cuts = [s[:, c * 128:(c + 1) * 128] for c in range(s.shape[1] // 128)]
            top = jnp.max(functools.reduce(jnp.maximum, cuts), axis=1, keepdims=True)
            old = m[a, h]
            new = jnp.maximum(old, top)
            m[a, h] = new
            fade = jnp.exp2((old - new) * scale2)
            probs = [jnp.exp2((c - new) * scale2) for c in cuts]
            l[a, h] = l[a, h] * fade + functools.reduce(jnp.add, probs)
            probs = jnp.concatenate([p.astype(jnp.bfloat16) for p in probs], axis=1)
            if pending is not None:
                finish(*pending)
            pending = (a, h, b, fade, probs)
        finish(*pending)

    def attend(queries, key_chunks):
        work = [(a, h, b) for b in key_chunks for a in queries for h in range(heads)]
        attend_block(work, 0, True)

        @pl.loop(1, 4)
        def _(dz):
            @pl.when(z >= dz)
            def _():
                attend_block(work, dz, False)

    m[...] = jnp.full(m.shape, NEG, jnp.float32)
    l[...] = jnp.zeros(l.shape, jnp.float32)
    acc[...] = jnp.zeros(acc.shape, jnp.float32)

    load_merged.wait()
    for j in range(NJ):
        project_image(j)
        if j == 0:
            pl.semaphore_wait(barrier, len(partners))
        send_windows(j)
        if j == 0:
            load_text.start()
            for c in load_w:
                c.start()
    load_text.wait()

    for u in range(AHEAD):
        place_windows(u)
        first(u)

    tasks = {}
    for i in range(NC):
        base = i * NJ + NJ
        tasks.setdefault(base + 1, []).append(functools.partial(project, i))
        if i > 0:
            tasks.setdefault(base + 2, []).append(
                functools.partial(attend, [i], list(range(i)))
            )
        tasks.setdefault(base + 2, []).insert(0, functools.partial(kv_one, i))
        tasks.setdefault(base + 3, []).append(functools.partial(kv_two, i))
        tasks.setdefault(base + 4, []).append(functools.partial(kv_three, i))
        tasks.setdefault(base + 4, []).append(
            functools.partial(attend, list(range(i + 1)), [i])
        )
    count = len(units)
    for u in range(max(count, max(tasks) + 1)):
        if u < count:
            second(u)
        if u + AHEAD < count:
            if u + AHEAD < NJ:
                place_windows(u + AHEAD)
            first(u + AHEAD)
        if 0 <= u - 1 < count:
            third(u - 1)
        if u == NJ:
            for c in load_w:
                c.wait()
        for task in tasks.get(u, []):
            task()

    for a in range(NC):
        for h in range(heads):
            total = jnp.sum(l[a, h], axis=1, keepdims=True)
            out[a * chunk:(a + 1) * chunk, h * HD:(h + 1) * HD] = (acc[a, h] / total).astype(
                jnp.bfloat16
            )

    for c in a_moves.values():
        c.wait_send()
    for c in moves.values():
        c.wait_send()
    for c, dz in kv_moves:
        if dz == 0:
            c.wait_send()
        else:
            @pl.when(z + dz <= 3)
            def _():
                c.wait_send()
    for i in range(NC):
        share(i, 0).wait_send()
        for dz in range(1, 4):
            @pl.when(z >= dz)
            def _():
                share(i, dz).wait_send()


def local(merged_hidden, counts, owner, down_proj, text_embed, norm_gain, w_query, w_key, w_value):
    rows, cols = text_embed.shape
    hidden = merged_hidden.shape[1]
    blocks = norm_gain.shape[0] // cols
    q_cols = w_query.shape[1]
    heads = q_cols // HD
    chunk = rows // NC
    any_space = pl.BlockSpec(memory_space=pl.ANY)
    vmem = pl.BlockSpec(memory_space=pltpu.VMEM)
    dma = pltpu.SemaphoreType.DMA
    return pl.pallas_call(
        layer_kernel,
        out_shape=jax.ShapeDtypeStruct((rows, q_cols), jnp.bfloat16),
        in_specs=[any_space] * 3 + [vmem] * 3 + [any_space] * 3,
        out_specs=vmem,
        scratch_shapes=[
            pltpu.VMEM((rows, hidden), jnp.bfloat16),
            pltpu.VMEM((NJ, hidden, cols // NJ), jnp.bfloat16),
            pltpu.VMEM((NJ, rows, cols // NJ), jnp.bfloat16),
            pltpu.VMEM((NJ, rows, cols // NJ), jnp.bfloat16),
            pltpu.VMEM((8, rows, cols), jnp.bfloat16),
            pltpu.VMEM((blocks, cols, q_cols), jnp.bfloat16),
            pltpu.VMEM((blocks, cols, 2 * HD), jnp.bfloat16),
            pltpu.VMEM((NC, heads, chunk, HD), jnp.bfloat16),
            pltpu.VMEM((NC, 4, 4 * chunk, 2 * HD), jnp.bfloat16),
            pltpu.VMEM((NC, heads, chunk, 128), jnp.float32),
            pltpu.VMEM((NC, heads, chunk, 128), jnp.float32),
            pltpu.VMEM((NC, heads, chunk, HD), jnp.float32),
            pltpu.VMEM((chunk, q_cols), jnp.float32),
            pltpu.VMEM((chunk, 2 * HD), jnp.float32),
            dma((2 + NJ,)),
            dma((3,)),
            dma((NJ, 16)),
            dma((NJ,)),
            dma((NC * NJ, 8)),
            dma((NC * NJ, 8)),
            dma((NC, 8)),
            dma((NC, 8)),
            dma((NC, 4)),
            dma((NC, 4)),
        ],
        compiler_params=pltpu.CompilerParams(
            collective_id=0, has_side_effects=True, vmem_limit_bytes=60 * 1024 * 1024
        ),
        name="layer",
    )(
        merged_hidden,
        down_proj,
        text_embed,
        counts.reshape(1, -1),
        owner,
        norm_gain.reshape(1, -1),
        w_query.reshape(blocks, cols, q_cols),
        w_key.reshape(blocks, cols, HD),
        w_value.reshape(blocks, cols, HD),
    )


def solution(mesh):
    in_specs = (
        P(("ctx", "grp"), None),
        P(),
        P(),
        P(None, "tp"),
        P(("ctx", "grp"), "tp"),
        P(),
        P(None, "tp"),
        P(None, "tp"),
        P(None, "tp"),
    )
    out_specs = P(("ctx", "grp"), "tp")
    return jax.shard_map(local, mesh=mesh, in_specs=in_specs, out_specs=out_specs, check_vma=False)
```

```python
import functools
import math

import jax
import jax.numpy as jnp
from jax import lax
from jax.experimental import pallas as pl
from jax.experimental.pallas import tpu as pltpu
from jax.sharding import PartitionSpec as P

HD = 128
NC = 8
NJ = 2
NK = 4
AHEAD = 3
MESH = pl.DeviceIdType.MESH
NEG = float("-inf")


def layer_kernel(
    merged_in, down_in, text_in, counts_in, owner_in, gain, wq_in, wk_in, wv_in, out,
    merged, down, image_sum, packed, arrived, seq, w, q, kv, ahead_by, m, l, acc,
    in_sem, w_sem, as_sem, ar_sem, gs, gr, ks, kr, fs, fr,
):
    rows, cols = text_in.shape
    shards, wcap = owner_in.shape
    window = rows // wcap
    most = wcap // shards
    part = cols // NJ
    depth = merged.shape[2]
    pair_rows = most * window
    chunk = rows // NC
    half = chunk // 2
    heads = q.shape[1] // chunk
    units = NC * NJ
    ctx = lax.axis_index("ctx")
    tp = lax.axis_index("tp")
    yh = lax.axis_index("grp")
    z, core = lax.div(ctx, 2), lax.rem(ctx, 2)
    yl, x = lax.div(tp, 4), lax.rem(tp, 4)
    rank = ctx * 2 + yh

    def at(dx, dy):
        return lax.rem(yl + dy, 2) * 4 + lax.rem(x + dx, 4)

    to_xp, to_xm, to_yp = {"tp": at(1, 0)}, {"tp": at(3, 0)}, {"tp": at(0, 1)}
    sibling = {"ctx": z * 2 + 1 - core}

    def shard_at(step):
        d = lax.rem(rank + step, shards)
        return d, {"ctx": lax.div(d, 2), "grp": lax.rem(d, 2)}

    barrier = pltpu.get_barrier_semaphore()
    partners = [to_xp, to_xm, to_yp] + [shard_at(n)[1] for n in range(1, shards)]
    for dev in partners:
        pl.semaphore_signal(barrier, inc=1, device_id=dev, device_id_type=MESH)

    def col(j):
        return pl.ds(j * part, part)

    loads = []
    for j in range(NJ):
        for k in range(NK):
            deep = pl.ds(k * depth, depth)
            stage = [
                pltpu.make_async_copy(
                    down_in.at[deep, col(j)], down.at[j, k], in_sem.at[j * NK + k]
                )
            ]
            if j == 0:
                stage.append(
                    pltpu.make_async_copy(
                        merged_in.at[:, deep], merged.at[k], in_sem.at[NJ * NK + k]
                    )
                )
            loads.append(stage)
    load_text = [
        pltpu.make_async_copy(text_in.at[:, col(j)], seq.at[0, j], in_sem.at[(NJ + 1) * NK + j])
        for j in range(NJ)
    ]
    load_w = [
        pltpu.make_async_copy(wk_in, w.at[:, :, pl.ds(0, HD)], w_sem.at[0]),
        pltpu.make_async_copy(wv_in, w.at[:, :, pl.ds(HD, HD)], w_sem.at[1]),
        pltpu.make_async_copy(wq_in, w.at[:, :, pl.ds(2 * HD, heads * HD)], w_sem.at[2]),
    ]
    loads.append(load_text)
    loads.append(load_w)
    for stage in loads[:3]:
        for c in stage:
            c.start()

    def remote(src, dst, ssem, rsem, dev):
        return pltpu.make_async_remote_copy(
            src_ref=src, dst_ref=dst, send_sem=ssem, recv_sem=rsem,
            device_id=dev, device_id_type=MESH,
        )

    def iota(shape, axis):
        return lax.broadcasted_iota(jnp.int32, shape, axis)

    shard_ids = iota((shards, wcap), 0)
    counts_col = jnp.sum(
        jnp.where(iota((shards, shards), 0) == iota((shards, shards), 1), counts_in[...], 0),
        axis=1, keepdims=True,
    )
    live = iota((shards, wcap), 1) < counts_col
    owner = owner_in[...]
    lane_win = lax.div(iota((wcap, rows), 1), window)
    spread = (lane_win == iota((wcap, rows), 0)).astype(jnp.float32)
    my_owner = jnp.sum(
        jnp.where(live & (shard_ids == rank), owner + 1, 0), axis=0, keepdims=True
    ).astype(jnp.float32)
    my_owner = jnp.broadcast_to(my_owner, (8, wcap))
    lane_owner = jnp.dot(my_owner, spread, preferred_element_type=jnp.float32)[:1].astype(jnp.int32)
    lane = iota((1, rows), 1)
    lane_slot = lax.div(lane, window * shards)
    slot_row = jnp.where(
        lane_owner > 0,
        (lane_owner - 1) * pair_rows + lane_slot * window + lax.rem(lane, window),
        -1,
    )
    arrivals = jnp.sum(
        (live & (owner == rank)).astype(jnp.int32), axis=1, keepdims=True
    )
    from_shard = lax.div(iota((shards, rows), 1), pair_rows)
    by_shard = iota((shards, rows), 0)
    before = jnp.sum(jnp.where(by_shard < from_shard, arrivals, 0), axis=0, keepdims=True)
    here = jnp.sum(jnp.where(by_shard == from_shard, arrivals, 0), axis=0, keepdims=True)
    pair_slot = lax.div(lax.rem(lane, pair_rows), window)
    dest_row = jnp.where(
        pair_slot < here, (before + pair_slot) * window + lax.rem(lane, window), -1
    )
    filled = jnp.sum(arrivals, axis=0, keepdims=True) * window
    row_ids = iota((rows, rows), 0)
    select = (row_ids == slot_row).astype(jnp.float32).astype(jnp.bfloat16)
    place = (row_ids == dest_row).astype(jnp.float32).astype(jnp.bfloat16)
    is_image = iota((rows, part), 0) < filled

    key = iota(ahead_by.shape, 1)
    dc, dy = lax.div(key, 2 * chunk), lax.rem(lax.div(key, chunk), 2)
    peer = jnp.where(dc == 0, core, 1 - core) * 2 + jnp.where(dy == 0, yh, 1 - yh)
    ahead_by[...] = (
        (peer - core * 2 - yh) * rows + lax.rem(key, chunk)
        - lax.rem(iota(ahead_by.shape, 0), chunk)
    )
    m[...] = jnp.full(m.shape, NEG, jnp.float32)
    l[...] = jnp.zeros(l.shape, jnp.float32)
    acc[...] = jnp.zeros(acc.shape, jnp.float32)

    def project_image(j):
        for k in range(NK):
            for c in loads[j * NK + k]:
                c.wait()
            if j * NK + k + 3 < len(loads):
                for c in loads[j * NK + k + 3]:
                    c.start()
            term = jnp.dot(merged[k], down[j, k], preferred_element_type=jnp.float32)
            if k == 0:
                image_sum[...] = term
            elif k < NK - 1:
                image_sum[...] += term
        image = (image_sum[...] + term).astype(jnp.bfloat16)
        packed[j] = jnp.dot(select, image, preferred_element_type=jnp.float32).astype(
            jnp.bfloat16
        )

    def own_pair():
        return pl.ds(pl.multiple_of(rank * pair_rows, pair_rows), pair_rows)

    a_moves = []

    def send_windows(j):
        for n in range(1, shards):
            d, dev = shard_at(n)
            there = pl.ds(pl.multiple_of(d * pair_rows, pair_rows), pair_rows)
            c = remote(
                packed.at[j, there], arrived.at[j, own_pair()], as_sem.at[j, n], ar_sem.at[j], dev
            )
            c.start()
            a_moves.append(c)
        arrived[j, own_pair(), :] = packed[j, own_pair(), :]

    def place_windows(j):
        others = pl.ds(0, (shards - 1) * pair_rows)
        remote(
            packed.at[j, others], arrived.at[j, others], as_sem.at[j, 0], ar_sem.at[j], sibling
        ).wait_recv()
        load_text[j].wait()
        placed = jnp.dot(place, arrived[j], preferred_element_type=jnp.float32)
        seq[0, j] = jnp.where(is_image, placed, seq[0, j].astype(jnp.float32)).astype(
            jnp.bfloat16
        )

    hops = {
        "own_y": (0, 3, 0, chunk, to_yp, 0),
        "own_xp": (0, 1, 0, chunk, to_xp, 1),
        "own_xm": (0, 2, 0, chunk, to_xm, 2),
        "opp_a": (1, 6, 0, half, to_xp, 3),
        "opp_b": (2, 6, half, half, to_xm, 4),
        "mate_xp": (3, 4, 0, chunk, to_xp, 5),
        "mate_xm": (3, 5, 0, chunk, to_xm, 6),
        "opp_y": (6, 7, 0, chunk, to_yp, 7),
    }

    def hop(u, name):
        src, dst, start, size, dev, index = hops[name]
        i, j = lax.div(u, NJ), lax.rem(u, NJ)
        r = pl.ds(pl.multiple_of(i * chunk + start, 16), size)
        return remote(
            seq.at[src, j, r], seq.at[dst, j, r], gs.at[u, index], gr.at[u, index], dev
        )

    def first(u):
        hop(u, "own_y").start()
        hop(u, "own_xp").start()
        hop(u, "own_xm").start()

    def second(u):
        hop(u, "own_xp").wait_recv()
        hop(u, "opp_a").start()
        hop(u, "own_xm").wait_recv()
        hop(u, "opp_b").start()
        hop(u, "own_y").wait_recv()
        hop(u, "mate_xp").start()
        hop(u, "mate_xm").start()

    def third(u):
        hop(u, "opp_a").wait_recv()
        hop(u, "opp_b").wait_recv()
        hop(u, "opp_y").start()

    places = [(0, 0), (3, 0), (1, 0), (0, 1), (3, 1), (1, 1), (2, 0), (2, 1)]

    def cut(dz, dc, dy, size):
        return pl.ds(((dz * 2 + dc) * 2 + dy) * chunk, size)

    def to_z(dz):
        return {"ctx": lax.rem(z + dz, 4) * 2 + core}

    def exchange(i):
        return remote(
            kv.at[i, cut(0, 0, 0, chunk)], kv.at[i, cut(0, 0, 1, chunk)],
            ks.at[i, 0], kr.at[i, 0], {"grp": 1 - yh},
        )

    def onward(i, dz, dy):
        index = 4 * dy + dz
        return remote(
            kv.at[i, cut(0, 0, dy, chunk)], kv.at[i, cut(dz, 0, dy, chunk)],
            ks.at[i, index], kr.at[i, index], to_z(dz),
        )

    def share(i, dz):
        return remote(
            kv.at[i, cut(dz, 0, 0, 2 * chunk)], kv.at[i, cut(dz, 1, 0, 2 * chunk)],
            fs.at[i, dz], fr.at[i, dz], sibling,
        )

    def project(i):
        r = pl.ds(pl.multiple_of(i * chunk, chunk), chunk)
        for j in range(NJ):
            for name in ("mate_xp", "mate_xm", "opp_y"):
                hop(i * NJ + j, name).wait_recv()

        def block(k):
            return jnp.concatenate([seq[k, j, r] for j in range(NJ)], axis=1).astype(jnp.float32)

        total = jnp.zeros((chunk, 128), jnp.float32)
        for k in range(8):
            v = block(k)
            squares = v * v
            for c in range(cols // 128):
                total = total + squares[:, c * 128:(c + 1) * 128]
        scale = lax.rsqrt(jnp.sum(total, axis=1, keepdims=True) / (8 * cols) + 1e-06)
        result = None
        for k in range(8):
            b = at(*places[k])
            g = gain[:, pl.ds(pl.multiple_of(b * cols, cols), cols)]
            normed = (block(k) * scale * g).astype(jnp.bfloat16)
            term = jnp.dot(normed, w[b], preferred_element_type=jnp.float32)
            result = term if result is None else result + term
        kv[i, cut(0, 0, 0, chunk)] = result[:, :2 * HD].astype(jnp.bfloat16)
        exchange(i).start()
        for dz in range(1, 4):
            @pl.when(z + dz <= 3)
            def _():
                onward(i, dz, 0).start()
        for h in range(heads):
            q[i, h * chunk:(h + 1) * chunk] = result[
                :, (h + 2) * HD:(h + 3) * HD
            ].astype(jnp.bfloat16)

    def kv_one(i):
        exchange(i).wait_recv()
        for dz in range(1, 4):
            @pl.when(z + dz <= 3)
            def _():
                onward(i, dz, 1).start()
        share(i, 0).start()

    def kv_two(i):
        for dz in range(1, 4):
            @pl.when(z >= dz)
            def _():
                onward(i, dz, 0).wait_recv()
                onward(i, dz, 1).wait_recv()
                share(i, dz).start()

    def kv_three(i):
        share(i, 0).wait_recv()
        for dz in range(1, 4):
            @pl.when(z >= dz)
            def _():
                share(i, dz).wait_recv()

    scale2 = math.log2(math.e) / math.sqrt(HD)
    tile = 2 * chunk

    def attend_tiles(pairs, keys):
        work = [(a, pl.ds(t * tile, tile), b) for a, b in pairs for t in range(q.shape[1] // tile)]

        def score(n):
            a, r, b = work[n]
            return lax.dot_general(
                q[a, r], kv[b, :keys, :HD], (((1,), (1,)), ((), ())),
                preferred_element_type=jnp.float32,
            )

        def finish(a, r, b, fade, probs):
            acc[a, r] = acc[a, r] * fade + jnp.dot(
                probs, kv[b, :keys, HD:], preferred_element_type=jnp.float32
            )

        coming = score(0)
        pending = None
        for n, (a, r, b) in enumerate(work):
            s = coming
            if n + 1 < len(work):
                coming = score(n + 1)
            cuts = [s[:, c * 128:(c + 1) * 128] for c in range(keys // 128)]
            for c in range(4 * chunk // 128):
                seen = ahead_by[:, c * 128:(c + 1) * 128] <= (a - b) * chunk
                cuts[c] = jnp.where(seen, cuts[c], NEG)
            top = jnp.max(functools.reduce(jnp.maximum, cuts), axis=1, keepdims=True)
            old = m[a, r]
            new = jnp.maximum(old, top)
            m[a, r] = new
            fade = jnp.exp2((old - new) * scale2)
            probs = [jnp.exp2((c - new) * scale2) for c in cuts]
            l[a, r] = l[a, r] * fade + functools.reduce(jnp.add, probs)
            probs = jnp.concatenate([p.astype(jnp.bfloat16) for p in probs], axis=1)
            if pending is not None:
                finish(*pending)
            pending = (a, r, b, fade, probs)
        finish(*pending)

    def attend(i, low, high):
        seen = jnp.minimum(i + 2, NC)

        def pair_of(n):
            column = n < seen
            return jnp.where(column, n, jnp.minimum(i + 1, NC - 1)), jnp.where(column, i, n - seen)

        for level in range(4):
            @pl.when(z == level)
            def _():
                @pl.loop(low, high)
                def _(p):
                    attend_tiles(
                        [pair_of(2 * p), pair_of(2 * p + 1)], (level + 1) * 4 * chunk
                    )

    for j in range(NJ):
        project_image(j)
        if j == 0:
            pl.semaphore_wait(barrier, len(partners))
        send_windows(j)
    early = [u for u in range(AHEAD) if u % NJ == 0]
    late = [u for u in range(AHEAD) if u % NJ]
    place_windows(0)
    for u in early:
        first(u)
    second(0)
    place_windows(1)
    for u in late:
        first(u)
    for c in load_w:
        c.wait()

    @pl.loop(0, 2 * NC + 7)
    def _(s):
        @pl.when(jnp.logical_and(s >= 1, s <= units))
        def _():
            third(s - 1)

        @pl.when(jnp.logical_and(s >= 1, s < units))
        def _():
            second(s)

        @pl.when(s + AHEAD < units)
        def _():
            first(s + AHEAD)

        odd = lax.rem(s, 2) == 1

        def chunk_at(lag):
            return lax.div(s - lag, 2)

        def due(lag, parity):
            return jnp.logical_and(
                parity, jnp.logical_and(s >= lag, s - lag <= 2 * (NC - 1))
            )

        even = jnp.logical_not(odd)

        @pl.when(due(4, even))
        def _():
            kv_one(chunk_at(4))

        @pl.when(due(6, even))
        def _():
            kv_two(chunk_at(6))

        @pl.when(due(3, odd))
        def _():
            project(chunk_at(3))

        @pl.when(due(7, odd))
        def _():
            kv_three(chunk_at(7))

        @pl.when(s >= 7)
        def _():
            i = lax.div(s - 7, 2)
            count = jnp.where(i == NC - 1, NC // 2, i + 1)
            cut_at = lax.div(count + 1, 2)
            attend(i, jnp.where(odd, 0, cut_at), jnp.where(odd, cut_at, count))

    for a in range(NC):
        total = jnp.sum(l[a], axis=1, keepdims=True)
        done = (acc[a] / total).astype(jnp.bfloat16)
        for h in range(heads):
            out[a * chunk:(a + 1) * chunk, h * HD:(h + 1) * HD] = done[h * chunk:(h + 1) * chunk]

    for c in a_moves:
        c.wait_send()

    @pl.loop(0, units)
    def _(u):
        for name in hops:
            hop(u, name).wait_send()

    @pl.loop(0, NC)
    def _(i):
        exchange(i).wait_send()
        share(i, 0).wait_send()
        for dz in range(1, 4):
            @pl.when(z + dz <= 3)
            def _():
                onward(i, dz, 0).wait_send()
                onward(i, dz, 1).wait_send()

            @pl.when(z >= dz)
            def _():
                share(i, dz).wait_send()


def local(merged_hidden, counts, owner, down_proj, text_embed, norm_gain, w_query, w_key, w_value):
    rows, cols = text_embed.shape
    hidden = merged_hidden.shape[1]
    blocks = norm_gain.shape[0] // cols
    q_cols = w_query.shape[1]
    heads = q_cols // HD
    chunk = rows // NC
    any_space = pl.BlockSpec(memory_space=pl.ANY)
    vmem = pl.BlockSpec(memory_space=pltpu.VMEM)
    dma = pltpu.SemaphoreType.DMA
    return pl.pallas_call(
        layer_kernel,
        out_shape=jax.ShapeDtypeStruct((rows, q_cols), jnp.bfloat16),
        in_specs=[any_space] * 3 + [vmem] * 3 + [any_space] * 3,
        out_specs=vmem,
        scratch_shapes=[
            pltpu.VMEM((NK, rows, hidden // NK), jnp.bfloat16),
            pltpu.VMEM((NJ, NK, hidden // NK, cols // NJ), jnp.bfloat16),
            pltpu.VMEM((rows, cols // NJ), jnp.float32),
            pltpu.VMEM((NJ, rows, cols // NJ), jnp.bfloat16),
            pltpu.VMEM((NJ, rows, cols // NJ), jnp.bfloat16),
            pltpu.VMEM((8, NJ, rows, cols // NJ), jnp.bfloat16),
            pltpu.VMEM((blocks, cols, q_cols + 2 * HD), jnp.bfloat16),
            pltpu.VMEM((NC, heads * chunk, HD), jnp.bfloat16),
            pltpu.VMEM((NC, 16 * chunk, 2 * HD), jnp.bfloat16),
            pltpu.VMEM((2 * chunk, 4 * chunk), jnp.int32),
            pltpu.VMEM((NC, heads * chunk, 128), jnp.float32),
            pltpu.VMEM((NC, heads * chunk, 128), jnp.float32),
            pltpu.VMEM((NC, heads * chunk, HD), jnp.float32),
            dma(((NJ + 1) * NK + NJ,)),
            dma((3,)),
            dma((NJ, 16)),
            dma((NJ,)),
            dma((NC * NJ, 8)),
            dma((NC * NJ, 8)),
            dma((NC, 8)),
            dma((NC, 8)),
            dma((NC, 4)),
            dma((NC, 4)),
        ],
        compiler_params=pltpu.CompilerParams(
            collective_id=0, has_side_effects=True, vmem_limit_bytes=60 * 1024 * 1024
        ),
        name="layer",
    )(
        merged_hidden,
        down_proj,
        text_embed,
        counts.reshape(1, -1),
        owner,
        norm_gain.reshape(1, -1),
        w_query.reshape(blocks, cols, q_cols),
        w_key.reshape(blocks, cols, HD),
        w_value.reshape(blocks, cols, HD),
    )


def solution(mesh):
    in_specs = (
        P(("ctx", "grp"), None),
        P(),
        P(),
        P(None, "tp"),
        P(("ctx", "grp"), "tp"),
        P(),
        P(None, "tp"),
        P(None, "tp"),
        P(None, "tp"),
    )
    out_specs = P(("ctx", "grp"), "tp")
    return jax.shard_map(local, mesh=mesh, in_specs=in_specs, out_specs=out_specs, check_vma=False)
```

```python
import functools
import math

import jax
import jax.numpy as jnp
from jax import lax
from jax.experimental import pallas as pl
from jax.experimental.pallas import tpu as pltpu
from jax.sharding import PartitionSpec as P

HD = 128
NC = 8
NJ = 2
NK = 4
AHEAD = 3
LATE = 3
MESH = pl.DeviceIdType.MESH
NEG = float("-inf")
LOWEST = -3e38


def layer_kernel(
    text_first, merged_in, down_in, text_in, counts_in, owner_in, gain, wq_in, wk_in, wv_in, out,
    merged, down, image_sum, packed, arrived, seq, w, q, kv, ahead_by, m, l, acc,
    in_sem, w_sem, as_sem, ar_sem, gs, gr, ks, kr, fs, fr,
):
    rows, cols = text_in.shape
    shards, wcap = owner_in.shape
    window = rows // wcap
    most = wcap // shards
    part = cols // NJ
    depth = merged.shape[2]
    pair_rows = most * window
    chunk = rows // NC
    half = chunk // 2
    heads = q.shape[1] // chunk
    units = NC * NJ
    lead = LATE if text_first else 0
    placed_rows = rows - lead * chunk

    def row_chunk(i):
        return lax.rem(i + NC - lead, NC)

    ctx = lax.axis_index("ctx")
    tp = lax.axis_index("tp")
    yh = lax.axis_index("grp")
    z, core = lax.div(ctx, 2), lax.rem(ctx, 2)
    yl, x = lax.div(tp, 4), lax.rem(tp, 4)
    rank = ctx * 2 + yh

    def at(dx, dy):
        return lax.rem(yl + dy, 2) * 4 + lax.rem(x + dx, 4)

    to_xp, to_xm, to_yp = {"tp": at(1, 0)}, {"tp": at(3, 0)}, {"tp": at(0, 1)}
    sibling = {"ctx": z * 2 + 1 - core}

    def shard_at(step):
        d = lax.rem(rank + step, shards)
        return d, {"ctx": lax.div(d, 2), "grp": lax.rem(d, 2)}

    barrier = pltpu.get_barrier_semaphore()
    partners = [to_xp, to_xm, to_yp] + [shard_at(n)[1] for n in range(1, shards)]
    for dev in partners:
        pl.semaphore_signal(barrier, inc=1, device_id=dev, device_id_type=MESH)

    def col(j):
        return pl.ds(j * part, part)

    loads = []
    for j in range(NJ):
        for k in range(NK):
            deep = pl.ds(k * depth, depth)
            stage = [
                pltpu.make_async_copy(
                    down_in.at[deep, col(j)], down.at[j, k], in_sem.at[j * NK + k]
                )
            ]
            if j == 0:
                stage.append(
                    pltpu.make_async_copy(
                        merged_in.at[:, deep], merged.at[k], in_sem.at[NJ * NK + k]
                    )
                )
            loads.append(stage)
    load_text = [
        pltpu.make_async_copy(text_in.at[:, col(j)], seq.at[0, j], in_sem.at[(NJ + 1) * NK + j])
        for j in range(NJ)
    ]
    load_w = [
        pltpu.make_async_copy(wk_in, w.at[:, :, pl.ds(0, HD)], w_sem.at[0]),
        pltpu.make_async_copy(wv_in, w.at[:, :, pl.ds(HD, HD)], w_sem.at[1]),
        pltpu.make_async_copy(wq_in, w.at[:, :, pl.ds(2 * HD, heads * HD)], w_sem.at[2]),
    ]
    loads.append([] if text_first else load_text)
    loads.append(load_w)
    if text_first:
        for c in load_text:
            c.start()
    for stage in loads[:3]:
        for c in stage:
            c.start()

    def remote(src, dst, ssem, rsem, dev):
        return pltpu.make_async_remote_copy(
            src_ref=src, dst_ref=dst, send_sem=ssem, recv_sem=rsem,
            device_id=dev, device_id_type=MESH,
        )

    def iota(shape, axis):
        return lax.broadcasted_iota(jnp.int32, shape, axis)

    shard_ids = iota((shards, wcap), 0)
    counts_col = jnp.sum(
        jnp.where(iota((shards, shards), 0) == iota((shards, shards), 1), counts_in[...], 0),
        axis=1, keepdims=True,
    )
    live = iota((shards, wcap), 1) < counts_col
    owner = owner_in[...]
    lane_win = lax.div(iota((wcap, rows), 1), window)
    spread = (lane_win == iota((wcap, rows), 0)).astype(jnp.float32)
    my_owner = jnp.sum(
        jnp.where(live & (shard_ids == rank), owner + 1, 0), axis=0, keepdims=True
    ).astype(jnp.float32)
    my_owner = jnp.broadcast_to(my_owner, (8, wcap))
    lane_owner = jnp.dot(my_owner, spread, preferred_element_type=jnp.float32)[:1].astype(jnp.int32)
    lane = iota((1, rows), 1)
    lane_slot = lax.div(lane, window * shards)
    slot_row = jnp.where(
        lane_owner > 0,
        (lane_owner - 1) * pair_rows + lane_slot * window + lax.rem(lane, window),
        -1,
    )
    arrivals = jnp.sum(
        (live & (owner == rank)).astype(jnp.int32), axis=1, keepdims=True
    )
    from_shard = lax.div(iota((shards, rows), 1), pair_rows)
    by_shard = iota((shards, rows), 0)
    before = jnp.sum(jnp.where(by_shard < from_shard, arrivals, 0), axis=0, keepdims=True)
    here = jnp.sum(jnp.where(by_shard == from_shard, arrivals, 0), axis=0, keepdims=True)
    pair_slot = lax.div(lax.rem(lane, pair_rows), window)
    dest_row = jnp.where(
        pair_slot < here, (before + pair_slot) * window + lax.rem(lane, window), -1
    )
    filled = jnp.sum(arrivals, axis=0, keepdims=True) * window
    row_ids = iota((rows, rows), 0)
    select = (row_ids == slot_row).astype(jnp.float32).astype(jnp.bfloat16)
    place = (row_ids == dest_row).astype(jnp.float32).astype(jnp.bfloat16)[:placed_rows]
    is_image = iota((placed_rows, part), 0) < filled

    key = iota(ahead_by.shape, 1)
    dc, dy = lax.div(key, 2 * chunk), lax.rem(lax.div(key, chunk), 2)
    peer = jnp.where(dc == 0, core, 1 - core) * 2 + jnp.where(dy == 0, yh, 1 - yh)
    ahead_by[...] = (
        (peer - core * 2 - yh) * rows + lax.rem(key, chunk)
        - lax.rem(iota(ahead_by.shape, 0), chunk)
    )
    m[...] = jnp.full(m.shape, LOWEST, jnp.float32)
    l[...] = jnp.zeros(l.shape, jnp.float32)
    acc[...] = jnp.zeros(acc.shape, jnp.float32)

    def project_image(j):
        for k in range(NK):
            for c in loads[j * NK + k]:
                c.wait()
            if j * NK + k + 3 < len(loads):
                for c in loads[j * NK + k + 3]:
                    c.start()
            term = jnp.dot(merged[k], down[j, k], preferred_element_type=jnp.float32)
            if k == 0:
                image_sum[...] = term
            elif k < NK - 1:
                image_sum[...] += term
        image = (image_sum[...] + term).astype(jnp.bfloat16)
        packed[j] = jnp.dot(select, image, preferred_element_type=jnp.float32).astype(
            jnp.bfloat16
        )

    def own_pair():
        return pl.ds(pl.multiple_of(rank * pair_rows, pair_rows), pair_rows)

    a_moves = []

    def send_windows(j):
        for n in range(1, shards):
            d, dev = shard_at(n)
            there = pl.ds(pl.multiple_of(d * pair_rows, pair_rows), pair_rows)
            c = remote(
                packed.at[j, there], arrived.at[j, own_pair()], as_sem.at[j, n], ar_sem.at[j], dev
            )
            c.start()
            a_moves.append(c)
        arrived[j, own_pair(), :] = packed[j, own_pair(), :]

    def place_windows(j):
        others = pl.ds(0, (shards - 1) * pair_rows)
        remote(
            packed.at[j, others], arrived.at[j, others], as_sem.at[j, 0], ar_sem.at[j], sibling
        ).wait_recv()
        if not text_first:
            load_text[j].wait()
        placed = jnp.dot(place, arrived[j], preferred_element_type=jnp.float32)
        text = seq[0, j, :placed_rows].astype(jnp.float32)
        seq[0, j, :placed_rows] = jnp.where(is_image, placed, text).astype(jnp.bfloat16)

    hops = {
        "own_y": (0, 3, 0, chunk, to_yp, 0),
        "own_xp": (0, 1, 0, chunk, to_xp, 1),
        "own_xm": (0, 2, 0, chunk, to_xm, 2),
        "opp_a": (1, 6, 0, half, to_xp, 3),
        "opp_b": (2, 6, half, half, to_xm, 4),
        "mate_xp": (3, 4, 0, chunk, to_xp, 5),
        "mate_xm": (3, 5, 0, chunk, to_xm, 6),
        "opp_y": (6, 7, 0, chunk, to_yp, 7),
    }

    def hop(u, name):
        src, dst, start, size, dev, index = hops[name]
        i, j = lax.div(u, NJ), lax.rem(u, NJ)
        r = pl.ds(pl.multiple_of(row_chunk(i) * chunk + start, 16), size)
        return remote(
            seq.at[src, j, r], seq.at[dst, j, r], gs.at[u, index], gr.at[u, index], dev
        )

    def first(u):
        hop(u, "own_y").start()
        hop(u, "own_xp").start()
        hop(u, "own_xm").start()

    def second(u):
        hop(u, "own_xp").wait_recv()
        hop(u, "opp_a").start()
        hop(u, "own_xm").wait_recv()
        hop(u, "opp_b").start()
        hop(u, "own_y").wait_recv()
        hop(u, "mate_xp").start()
        hop(u, "mate_xm").start()

    def third(u):
        hop(u, "opp_a").wait_recv()
        hop(u, "opp_b").wait_recv()
        hop(u, "opp_y").start()

    places = [(0, 0), (3, 0), (1, 0), (0, 1), (3, 1), (1, 1), (2, 0), (2, 1)]

    def cut(dz, dc, dy, size):
        return pl.ds(((dz * 2 + dc) * 2 + dy) * chunk, size)

    def to_z(dz):
        return {"ctx": lax.rem(z + dz, 4) * 2 + core}

    def exchange(i):
        return remote(
            kv.at[i, cut(0, 0, 0, chunk)], kv.at[i, cut(0, 0, 1, chunk)],
            ks.at[i, 0], kr.at[i, 0], {"grp": 1 - yh},
        )

    def onward(i, dz, dy):
        index = 4 * dy + dz
        return remote(
            kv.at[i, cut(0, 0, dy, chunk)], kv.at[i, cut(dz, 0, dy, chunk)],
            ks.at[i, index], kr.at[i, index], to_z(dz),
        )

    def share(i, dz):
        return remote(
            kv.at[i, cut(dz, 0, 0, 2 * chunk)], kv.at[i, cut(dz, 1, 0, 2 * chunk)],
            fs.at[i, dz], fr.at[i, dz], sibling,
        )

    def project(i):
        r = pl.ds(pl.multiple_of(row_chunk(i) * chunk, chunk), chunk)
        for j in range(NJ):
            for name in ("mate_xp", "mate_xm", "opp_y"):
                hop(i * NJ + j, name).wait_recv()

        def block(k):
            return jnp.concatenate([seq[k, j, r] for j in range(NJ)], axis=1).astype(jnp.float32)

        total = jnp.zeros((chunk, 128), jnp.float32)
        for k in range(8):
            v = block(k)
            squares = v * v
            for c in range(cols // 128):
                total = total + squares[:, c * 128:(c + 1) * 128]
        scale = lax.rsqrt(jnp.sum(total, axis=1, keepdims=True) / (8 * cols) + 1e-06)
        result = None
        for k in range(8):
            b = at(*places[k])
            g = gain[:, pl.ds(pl.multiple_of(b * cols, cols), cols)]
            normed = (block(k) * scale * g).astype(jnp.bfloat16)
            term = jnp.dot(normed, w[b], preferred_element_type=jnp.float32)
            result = term if result is None else result + term
        kv[i, cut(0, 0, 0, chunk)] = result[:, :2 * HD].astype(jnp.bfloat16)
        exchange(i).start()
        for dz in range(1, 4):
            @pl.when(z + dz <= 3)
            def _():
                onward(i, dz, 0).start()
        for h in range(heads):
            q[i, h * chunk:(h + 1) * chunk] = result[
                :, (h + 2) * HD:(h + 3) * HD
            ].astype(jnp.bfloat16)

    def kv_one(i):
        exchange(i).wait_recv()
        for dz in range(1, 4):
            @pl.when(z + dz <= 3)
            def _():
                onward(i, dz, 1).start()
        share(i, 0).start()

    def kv_two(i):
        for dz in range(1, 4):
            @pl.when(z >= dz)
            def _():
                onward(i, dz, 0).wait_recv()
                onward(i, dz, 1).wait_recv()
                share(i, dz).start()

    def kv_three(i):
        share(i, 0).wait_recv()
        for dz in range(1, 4):
            @pl.when(z >= dz)
            def _():
                share(i, dz).wait_recv()

    scale2 = math.log2(math.e) / math.sqrt(HD)
    tile = 2 * chunk

    def attend_tiles(pairs, keys):
        work = [(a, pl.ds(t * tile, tile), b) for a, b in pairs for t in range(q.shape[1] // tile)]

        def score(n):
            a, r, b = work[n]
            return lax.dot_general(
                q[a, r], kv[b, :keys, :HD], (((1,), (1,)), ((), ())),
                preferred_element_type=jnp.float32,
            )

        def finish(a, r, b, fade, probs):
            acc[a, r] = acc[a, r] * fade + jnp.dot(
                probs, kv[b, :keys, HD:], preferred_element_type=jnp.float32
            )

        coming = score(0)
        pending = None
        for n, (a, r, b) in enumerate(work):
            s = coming
            if n + 1 < len(work):
                coming = score(n + 1)
            cuts = [s[:, c * 128:(c + 1) * 128] for c in range(keys // 128)]
            for c in range(4 * chunk // 128):
                seen = ahead_by[:, c * 128:(c + 1) * 128] <= (row_chunk(a) - row_chunk(b)) * chunk
                cuts[c] = jnp.where(seen, cuts[c], NEG)
            top = jnp.max(functools.reduce(jnp.maximum, cuts), axis=1, keepdims=True)
            old = m[a, r]
            new = jnp.maximum(old, top)
            m[a, r] = new
            fade = jnp.exp2((old - new) * scale2)
            probs = [jnp.exp2((c - new) * scale2) for c in cuts]
            l[a, r] = l[a, r] * fade + functools.reduce(jnp.add, probs)
            probs = jnp.concatenate([p.astype(jnp.bfloat16) for p in probs], axis=1)
            if pending is not None:
                finish(*pending)
            pending = (a, r, b, fade, probs)
        finish(*pending)

    def attend(i, low, high):
        seen = jnp.minimum(i + 2, NC)

        def pair_of(n):
            column = n < seen
            return jnp.where(column, n, jnp.minimum(i + 1, NC - 1)), jnp.where(column, i, n - seen)

        fours = lax.div(high - low, 2)
        for level in range(4):
            keys = (level + 1) * 4 * chunk

            @pl.when(z == level)
            def _():
                @pl.loop(0, fours)
                def _(t):
                    at_pair = 2 * (low + 2 * t)
                    attend_tiles([pair_of(at_pair + n) for n in range(4)], keys)

                @pl.when(high - low > 2 * fours)
                def _():
                    attend_tiles([pair_of(2 * high - 2), pair_of(2 * high - 1)], keys)

    def forwards(s):
        @pl.when(jnp.logical_and(s >= 1, s <= units))
        def _():
            third(s - 1)

        @pl.when(s < units)
        def _():
            second(s)

        @pl.when(s + AHEAD < units)
        def _():
            first(s + AHEAD)

    if text_first:
        for c in load_text:
            c.wait()
        pl.semaphore_wait(barrier, len(partners))
        for u in range(AHEAD):
            first(u)
        project_image(0)
        send_windows(0)
        second(0)
        first(AHEAD)
        project_image(1)
        send_windows(1)
        third(0)
        second(1)
        first(AHEAD + 1)
        third(1)
        second(2)
        for c in load_w:
            c.wait()
        place_windows(0)
        place_windows(1)
        first(AHEAD + 2)
    else:
        for j in range(NJ):
            project_image(j)
            if j == 0:
                pl.semaphore_wait(barrier, len(partners))
            send_windows(j)
        early = [u for u in range(AHEAD + 2) if u % NJ == 0]
        late = [u for u in range(AHEAD + 2) if u % NJ]
        place_windows(0)
        for u in early:
            first(u)
        second(0)
        place_windows(1)
        for u in late:
            first(u)
        for c in load_w:
            c.wait()
        third(0)
        second(1)
        third(1)
        second(2)
        first(AHEAD + 2)

    @pl.loop(3, 2 * NC + 6)
    def _(s):
        forwards(s)
        odd = lax.rem(s, 2) == 1
        even = jnp.logical_not(odd)

        def chunk_at(lag):
            return lax.div(s - lag, 2)

        def due(lag, parity):
            return jnp.logical_and(
                parity, jnp.logical_and(s >= lag, s - lag <= 2 * (NC - 1))
            )

        @pl.when(due(5, odd))
        def _():
            kv_two(chunk_at(5))

        @pl.when(due(3, odd))
        def _():
            project(chunk_at(3))

        @pl.when(due(4, even))
        def _():
            kv_one(chunk_at(4))

        @pl.when(due(6, even))
        def _():
            kv_three(chunk_at(6))

        @pl.when(s >= 6)
        def _():
            i = lax.div(s - 6, 2)
            count = jnp.where(i == NC - 1, NC // 2, i + 1)
            half_way = jnp.minimum(2 * lax.div(lax.div(count + 1, 2) + 1, 2), count)
            attend(i, jnp.where(odd, half_way, 0), jnp.where(odd, count, half_way))

    for a in range(NC):
        total = jnp.sum(l[a], axis=1, keepdims=True)
        done = (acc[a] / total).astype(jnp.bfloat16)
        start = (a + NC - lead) % NC * chunk
        for h in range(heads):
            out[pl.ds(start, chunk), h * HD:(h + 1) * HD] = done[h * chunk:(h + 1) * chunk]

    for c in a_moves:
        c.wait_send()

    @pl.loop(0, units)
    def _(u):
        for name in hops:
            hop(u, name).wait_send()

    @pl.loop(0, NC)
    def _(i):
        exchange(i).wait_send()
        share(i, 0).wait_send()
        for dz in range(1, 4):
            @pl.when(z + dz <= 3)
            def _():
                onward(i, dz, 0).wait_send()
                onward(i, dz, 1).wait_send()

            @pl.when(z >= dz)
            def _():
                share(i, dz).wait_send()


def layer(text_first, *operands):
    rows, cols = operands[2].shape
    hidden = operands[0].shape[1]
    blocks, _, q_cols = operands[6].shape
    heads = q_cols // HD
    chunk = rows // NC
    any_space = pl.BlockSpec(memory_space=pl.ANY)
    vmem = pl.BlockSpec(memory_space=pltpu.VMEM)
    dma = pltpu.SemaphoreType.DMA
    return pl.pallas_call(
        functools.partial(layer_kernel, text_first),
        out_shape=jax.ShapeDtypeStruct((rows, q_cols), jnp.bfloat16),
        in_specs=[any_space] * 3 + [vmem] * 3 + [any_space] * 3,
        out_specs=vmem,
        scratch_shapes=[
            pltpu.VMEM((NK, rows, hidden // NK), jnp.bfloat16),
            pltpu.VMEM((NJ, NK, hidden // NK, cols // NJ), jnp.bfloat16),
            pltpu.VMEM((rows, cols // NJ), jnp.float32),
            pltpu.VMEM((NJ, rows, cols // NJ), jnp.bfloat16),
            pltpu.VMEM((NJ, rows, cols // NJ), jnp.bfloat16),
            pltpu.VMEM((8, NJ, rows, cols // NJ), jnp.bfloat16),
            pltpu.VMEM((blocks, cols, q_cols + 2 * HD), jnp.bfloat16),
            pltpu.VMEM((NC, heads * chunk, HD), jnp.bfloat16),
            pltpu.VMEM((NC, 16 * chunk, 2 * HD), jnp.bfloat16),
            pltpu.VMEM((2 * chunk, 4 * chunk), jnp.int32),
            pltpu.VMEM((NC, heads * chunk, 128), jnp.float32),
            pltpu.VMEM((NC, heads * chunk, 128), jnp.float32),
            pltpu.VMEM((NC, heads * chunk, HD), jnp.float32),
            dma(((NJ + 1) * NK + NJ,)),
            dma((3,)),
            dma((NJ, 16)),
            dma((NJ,)),
            dma((NC * NJ, 8)),
            dma((NC * NJ, 8)),
            dma((NC, 8)),
            dma((NC, 8)),
            dma((NC, 4)),
            dma((NC, 4)),
        ],
        compiler_params=pltpu.CompilerParams(
            collective_id=int(text_first), has_side_effects=True, vmem_limit_bytes=60 * 1024 * 1024
        ),
        name="layer_text_first" if text_first else "layer",
    )(*operands)


def local(merged_hidden, counts, owner, down_proj, text_embed, norm_gain, w_query, w_key, w_value):
    rows, cols = text_embed.shape
    shards, wcap = owner.shape
    blocks = norm_gain.shape[0] // cols
    q_cols = w_query.shape[1]
    live = jnp.arange(wcap, dtype=jnp.int32)[None, :] < counts[:, None]
    ids = jnp.arange(shards, dtype=jnp.int32)
    hits = (owner[:, :, None] == ids) & live[:, :, None]
    fullest = jnp.max(jnp.sum(hits.astype(jnp.int32), axis=(0, 1)))
    text_first = fullest * (rows // wcap) <= rows - LATE * (rows // NC)
    return lax.cond(
        text_first,
        functools.partial(layer, True),
        functools.partial(layer, False),
        merged_hidden,
        down_proj,
        text_embed,
        counts.reshape(1, -1),
        owner,
        norm_gain.reshape(1, -1),
        w_query.reshape(blocks, cols, q_cols),
        w_key.reshape(blocks, cols, HD),
        w_value.reshape(blocks, cols, HD),
    )


def solution(mesh):
    in_specs = (
        P(("ctx", "grp"), None),
        P(),
        P(),
        P(None, "tp"),
        P(("ctx", "grp"), "tp"),
        P(),
        P(None, "tp"),
        P(None, "tp"),
        P(None, "tp"),
    )
    out_specs = P(("ctx", "grp"), "tp")
    return jax.shard_map(local, mesh=mesh, in_specs=in_specs, out_specs=out_specs, check_vma=False)
```

```python
import functools
import math

import jax
import jax.numpy as jnp
from jax import lax
from jax.experimental import pallas as pl
from jax.experimental.pallas import tpu as pltpu
from jax.sharding import PartitionSpec as P

HD = 128
NC = 8
NJ = 2
NK = 4
AHEAD = 3
LATE = 3
MESH = pl.DeviceIdType.MESH
NEG = float("-inf")
LOWEST = -3e38


def layer_kernel(
    text_first, merged_in, down_in, text_in, counts_in, owner_in, gain, wq_in, wk_in, wv_in, out,
    merged, down, image_sum, packed, arrived, seq, w, q, kv, ahead_by, m, l, acc,
    in_sem, w_sem, as_sem, ar_sem, gs, gr, ks, kr, fs, fr,
):
    rows, cols = text_in.shape
    shards, wcap = owner_in.shape
    window = rows // wcap
    most = wcap // shards
    part = cols // NJ
    depth = merged.shape[2]
    pair_rows = most * window
    chunk = rows // NC
    half = chunk // 2
    heads = q.shape[1] // chunk
    units = NC * NJ
    lead = LATE if text_first else 0
    placed_rows = rows - lead * chunk

    def row_chunk(i):
        return lax.rem(i + NC - lead, NC)

    ctx = lax.axis_index("ctx")
    tp = lax.axis_index("tp")
    yh = lax.axis_index("grp")
    z, core = lax.div(ctx, 2), lax.rem(ctx, 2)
    yl, x = lax.div(tp, 4), lax.rem(tp, 4)
    rank = ctx * 2 + yh

    def at(dx, dy):
        return lax.rem(yl + dy, 2) * 4 + lax.rem(x + dx, 4)

    to_xp, to_xm, to_yp = {"tp": at(1, 0)}, {"tp": at(3, 0)}, {"tp": at(0, 1)}
    sibling = {"ctx": z * 2 + 1 - core}

    def shard_at(step):
        d = lax.rem(rank + step, shards)
        return d, {"ctx": lax.div(d, 2), "grp": lax.rem(d, 2)}

    barrier = pltpu.get_barrier_semaphore()
    partners = [to_xp, to_xm, to_yp] + [shard_at(n)[1] for n in range(1, shards)]
    for dev in partners:
        pl.semaphore_signal(barrier, inc=1, device_id=dev, device_id_type=MESH)

    def col(j):
        return pl.ds(j * part, part)

    loads = []
    for j in range(NJ):
        for k in range(NK):
            deep = pl.ds(k * depth, depth)
            stage = [
                pltpu.make_async_copy(
                    down_in.at[deep, col(j)], down.at[j, k], in_sem.at[j * NK + k]
                )
            ]
            if j == 0:
                stage.append(
                    pltpu.make_async_copy(
                        merged_in.at[:, deep], merged.at[k], in_sem.at[NJ * NK + k]
                    )
                )
            loads.append(stage)
    load_text = [
        pltpu.make_async_copy(text_in.at[:, col(j)], seq.at[0, j], in_sem.at[(NJ + 1) * NK + j])
        for j in range(NJ)
    ]
    load_w = [
        pltpu.make_async_copy(wk_in, w.at[:, :, pl.ds(0, HD)], w_sem.at[0]),
        pltpu.make_async_copy(wv_in, w.at[:, :, pl.ds(HD, HD)], w_sem.at[1]),
        pltpu.make_async_copy(wq_in, w.at[:, :, pl.ds(2 * HD, heads * HD)], w_sem.at[2]),
    ]
    loads.append([] if text_first else load_text)
    loads.append(load_w)
    if text_first:
        for c in load_text:
            c.start()
    for stage in loads[:3]:
        for c in stage:
            c.start()

    def remote(src, dst, ssem, rsem, dev):
        return pltpu.make_async_remote_copy(
            src_ref=src, dst_ref=dst, send_sem=ssem, recv_sem=rsem,
            device_id=dev, device_id_type=MESH,
        )

    def iota(shape, axis):
        return lax.broadcasted_iota(jnp.int32, shape, axis)

    shard_ids = iota((shards, wcap), 0)
    counts_col = jnp.sum(
        jnp.where(iota((shards, shards), 0) == iota((shards, shards), 1), counts_in[...], 0),
        axis=1, keepdims=True,
    )
    live = iota((shards, wcap), 1) < counts_col
    owner = owner_in[...]
    lane_win = lax.div(iota((wcap, rows), 1), window)
    spread = (lane_win == iota((wcap, rows), 0)).astype(jnp.float32)
    my_owner = jnp.sum(
        jnp.where(live & (shard_ids == rank), owner + 1, 0), axis=0, keepdims=True
    ).astype(jnp.float32)
    my_owner = jnp.broadcast_to(my_owner, (8, wcap))
    lane_owner = jnp.dot(my_owner, spread, preferred_element_type=jnp.float32)[:1].astype(jnp.int32)
    lane = iota((1, rows), 1)
    lane_slot = lax.div(lane, window * shards)
    slot_row = jnp.where(
        lane_owner > 0,
        (lane_owner - 1) * pair_rows + lane_slot * window + lax.rem(lane, window),
        -1,
    )
    arrivals = jnp.sum(
        (live & (owner == rank)).astype(jnp.int32), axis=1, keepdims=True
    )
    from_shard = lax.div(iota((shards, rows), 1), pair_rows)
    by_shard = iota((shards, rows), 0)
    before = jnp.sum(jnp.where(by_shard < from_shard, arrivals, 0), axis=0, keepdims=True)
    here = jnp.sum(jnp.where(by_shard == from_shard, arrivals, 0), axis=0, keepdims=True)
    pair_slot = lax.div(lax.rem(lane, pair_rows), window)
    dest_row = jnp.where(
        pair_slot < here, (before + pair_slot) * window + lax.rem(lane, window), -1
    )
    filled = jnp.sum(arrivals, axis=0, keepdims=True) * window
    row_ids = iota((rows, rows), 0)
    select = (row_ids == slot_row).astype(jnp.float32).astype(jnp.bfloat16)
    place = (row_ids == dest_row).astype(jnp.float32).astype(jnp.bfloat16)[:placed_rows]
    is_image = iota((placed_rows, part), 0) < filled

    key = iota(ahead_by.shape, 1)
    dc, dy = lax.div(key, 2 * chunk), lax.rem(lax.div(key, chunk), 2)
    peer = jnp.where(dc == 0, core, 1 - core) * 2 + jnp.where(dy == 0, yh, 1 - yh)
    ahead_by[...] = (
        (peer - core * 2 - yh) * rows + lax.rem(key, chunk)
        - lax.rem(iota(ahead_by.shape, 0), chunk)
    )
    m[...] = jnp.full(m.shape, LOWEST, jnp.float32)
    l[...] = jnp.zeros(l.shape, jnp.float32)
    acc[...] = jnp.zeros(acc.shape, jnp.float32)

    def project_image(j):
        for k in range(NK):
            for c in loads[j * NK + k]:
                c.wait()
            if j * NK + k + 3 < len(loads):
                for c in loads[j * NK + k + 3]:
                    c.start()
            term = jnp.dot(merged[k], down[j, k], preferred_element_type=jnp.float32)
            if k == 0:
                image_sum[...] = term
            elif k < NK - 1:
                image_sum[...] += term
        image = (image_sum[...] + term).astype(jnp.bfloat16)
        packed[j] = jnp.dot(select, image, preferred_element_type=jnp.float32).astype(
            jnp.bfloat16
        )

    def own_pair():
        return pl.ds(pl.multiple_of(rank * pair_rows, pair_rows), pair_rows)

    a_moves = []

    def send_windows(j):
        for n in range(1, shards):
            d, dev = shard_at(n)
            there = pl.ds(pl.multiple_of(d * pair_rows, pair_rows), pair_rows)
            c = remote(
                packed.at[j, there], arrived.at[j, own_pair()], as_sem.at[j, n], ar_sem.at[j], dev
            )
            c.start()
            a_moves.append(c)
        arrived[j, own_pair(), :] = packed[j, own_pair(), :]

    def place_windows(j):
        others = pl.ds(0, (shards - 1) * pair_rows)
        remote(
            packed.at[j, others], arrived.at[j, others], as_sem.at[j, 0], ar_sem.at[j], sibling
        ).wait_recv()
        if not text_first:
            load_text[j].wait()
        placed = jnp.dot(place, arrived[j], preferred_element_type=jnp.float32)
        text = seq[0, j, :placed_rows].astype(jnp.float32)
        seq[0, j, :placed_rows] = jnp.where(is_image, placed, text).astype(jnp.bfloat16)

    hops = {
        "own_y": (0, 3, 0, chunk, to_yp, 0),
        "own_xp": (0, 1, 0, chunk, to_xp, 1),
        "own_xm": (0, 2, 0, chunk, to_xm, 2),
        "opp_a": (1, 6, 0, half, to_xp, 3),
        "opp_b": (2, 6, half, half, to_xm, 4),
        "mate_xp": (3, 4, 0, chunk, to_xp, 5),
        "mate_xm": (3, 5, 0, chunk, to_xm, 6),
        "opp_y": (6, 7, 0, chunk, to_yp, 7),
    }

    def hop(u, name):
        src, dst, start, size, dev, index = hops[name]
        i, j = lax.div(u, NJ), lax.rem(u, NJ)
        r = pl.ds(pl.multiple_of(row_chunk(i) * chunk + start, 16), size)
        return remote(
            seq.at[src, j, r], seq.at[dst, j, r], gs.at[u, index], gr.at[u, index], dev
        )

    def first(u):
        hop(u, "own_y").start()
        hop(u, "own_xp").start()
        hop(u, "own_xm").start()

    def second(u):
        hop(u, "own_xp").wait_recv()
        hop(u, "opp_a").start()
        hop(u, "own_xm").wait_recv()
        hop(u, "opp_b").start()
        hop(u, "own_y").wait_recv()
        hop(u, "mate_xp").start()
        hop(u, "mate_xm").start()

    def third(u):
        hop(u, "opp_a").wait_recv()
        hop(u, "opp_b").wait_recv()
        hop(u, "opp_y").start()

    places = [(0, 0), (3, 0), (1, 0), (0, 1), (3, 1), (1, 1), (2, 0), (2, 1)]

    def cut(dz, dc, dy, size):
        return pl.ds(((dz * 2 + dc) * 2 + dy) * chunk, size)

    def to_z(dz):
        return {"ctx": lax.rem(z + dz, 4) * 2 + core}

    def exchange(i):
        return remote(
            kv.at[i, cut(0, 0, 0, chunk)], kv.at[i, cut(0, 0, 1, chunk)],
            ks.at[i, 0], kr.at[i, 0], {"grp": 1 - yh},
        )

    def onward(i, dz, dy):
        index = 4 * dy + dz
        return remote(
            kv.at[i, cut(0, 0, dy, chunk)], kv.at[i, cut(dz, 0, dy, chunk)],
            ks.at[i, index], kr.at[i, index], to_z(dz),
        )

    def share(i, dz):
        return remote(
            kv.at[i, cut(dz, 0, 0, 2 * chunk)], kv.at[i, cut(dz, 1, 0, 2 * chunk)],
            fs.at[i, dz], fr.at[i, dz], sibling,
        )

    def project(i):
        r = pl.ds(pl.multiple_of(row_chunk(i) * chunk, chunk), chunk)
        for j in range(NJ):
            for name in ("mate_xp", "mate_xm", "opp_y"):
                hop(i * NJ + j, name).wait_recv()

        def block(k):
            return jnp.concatenate([seq[k, j, r] for j in range(NJ)], axis=1).astype(jnp.float32)

        total = jnp.zeros((chunk, 128), jnp.float32)
        for k in range(8):
            v = block(k)
            squares = v * v
            for c in range(cols // 128):
                total = total + squares[:, c * 128:(c + 1) * 128]
        scale = lax.rsqrt(jnp.sum(total, axis=1, keepdims=True) / (8 * cols) + 1e-06)
        result = None
        for k in range(8):
            b = at(*places[k])
            g = gain[:, pl.ds(pl.multiple_of(b * cols, cols), cols)]
            normed = (block(k) * scale * g).astype(jnp.bfloat16)
            term = jnp.dot(normed, w[b], preferred_element_type=jnp.float32)
            result = term if result is None else result + term
        kv[i, cut(0, 0, 0, chunk)] = result[:, :2 * HD].astype(jnp.bfloat16)
        exchange(i).start()
        for dz in range(1, 4):
            @pl.when(z + dz <= 3)
            def _():
                onward(i, dz, 0).start()
        for h in range(heads):
            q[i, h * chunk:(h + 1) * chunk] = result[
                :, (h + 2) * HD:(h + 3) * HD
            ].astype(jnp.bfloat16)

    def kv_one(i):
        exchange(i).wait_recv()
        for dz in range(1, 4):
            @pl.when(z + dz <= 3)
            def _():
                onward(i, dz, 1).start()
        share(i, 0).start()

    def kv_two(i):
        for dz in range(1, 4):
            @pl.when(z >= dz)
            def _():
                onward(i, dz, 0).wait_recv()
                onward(i, dz, 1).wait_recv()
                share(i, dz).start()

    def kv_three(i):
        share(i, 0).wait_recv()
        for dz in range(1, 4):
            @pl.when(z >= dz)
            def _():
                share(i, dz).wait_recv()

    scale2 = math.log2(math.e) / math.sqrt(HD)
    tile = 2 * chunk

    def attend_tiles(pairs, keys):
        work = [(a, pl.ds(t * tile, tile), b) for a, b in pairs for t in range(q.shape[1] // tile)]

        def score(n):
            a, r, b = work[n]
            return lax.dot_general(
                q[a, r], kv[b, :keys, :HD], (((1,), (1,)), ((), ())),
                preferred_element_type=jnp.float32,
            )

        def finish(a, r, b, fade, probs):
            acc[a, r] = acc[a, r] * fade + jnp.dot(
                probs, kv[b, :keys, HD:], preferred_element_type=jnp.float32
            )

        coming = score(0)
        pending = None
        for n, (a, r, b) in enumerate(work):
            s = coming
            if n + 1 < len(work):
                coming = score(n + 1)
            cuts = [s[:, c * 128:(c + 1) * 128] for c in range(keys // 128)]
            for c in range(4 * chunk // 128):
                seen = ahead_by[:, c * 128:(c + 1) * 128] <= (row_chunk(a) - row_chunk(b)) * chunk
                cuts[c] = jnp.where(seen, cuts[c], NEG)
            top = jnp.max(functools.reduce(jnp.maximum, cuts), axis=1, keepdims=True)
            old = m[a, r]
            new = jnp.maximum(old, top)
            m[a, r] = new
            fade = jnp.exp2((old - new) * scale2)
            probs = [jnp.exp2((c - new) * scale2) for c in cuts]
            l[a, r] = l[a, r] * fade + functools.reduce(jnp.add, probs)
            probs = jnp.concatenate([p.astype(jnp.bfloat16) for p in probs], axis=1)
            if pending is not None:
                finish(*pending)
            pending = (a, r, b, fade, probs)
        finish(*pending)

    def attend(i, low, high):
        seen = jnp.minimum(i + 2, NC)

        def pair_of(n):
            column = n < seen
            return jnp.where(column, n, jnp.minimum(i + 1, NC - 1)), jnp.where(column, i, n - seen)

        fours = lax.div(high - low, 2)
        for level in range(4):
            keys = (level + 1) * 4 * chunk

            @pl.when(z == level)
            def _():
                @pl.loop(0, fours)
                def _(t):
                    at_pair = 2 * (low + 2 * t)
                    attend_tiles([pair_of(at_pair + n) for n in range(4)], keys)

                @pl.when(high - low > 2 * fours)
                def _():
                    attend_tiles([pair_of(2 * high - 2), pair_of(2 * high - 1)], keys)

    def forwards(s):
        @pl.when(s <= units)
        def _():
            third(s - 1)

        @pl.when(jnp.logical_and(s >= 4, s < units))
        def _():
            second(s)

        @pl.when(s + AHEAD < units)
        def _():
            first(s + AHEAD)

    if text_first:
        for c in load_text:
            c.wait()
        pl.semaphore_wait(barrier, len(partners))
        for u in range(LATE * NJ):
            first(u)
        project_image(0)
        send_windows(0)
        second(0)
        second(1)
        project_image(1)
        send_windows(1)
        third(0)
        third(1)
        second(2)
        second(3)
        for c in load_w:
            c.wait()
        place_windows(0)
        place_windows(1)
    else:
        for j in range(NJ):
            project_image(j)
            if j == 0:
                pl.semaphore_wait(barrier, len(partners))
            send_windows(j)
        early = [u for u in range(AHEAD + 2) if u % NJ == 0]
        late = [u for u in range(AHEAD + 2) if u % NJ]
        place_windows(0)
        for u in early:
            first(u)
        second(0)
        place_windows(1)
        for u in late:
            first(u)
        for c in load_w:
            c.wait()
        third(0)
        second(1)
        third(1)
        second(2)
        first(AHEAD + 2)
        second(3)

    @pl.loop(3, 2 * NC + 6)
    def _(s):
        forwards(s)
        odd = lax.rem(s, 2) == 1
        even = jnp.logical_not(odd)

        def chunk_at(lag):
            return lax.div(s - lag, 2)

        def due(lag, parity):
            return jnp.logical_and(
                parity, jnp.logical_and(s >= lag, s - lag <= 2 * (NC - 1))
            )

        @pl.when(due(3, odd))
        def _():
            project(chunk_at(3))

        @pl.when(due(6, even))
        def _():
            kv_three(chunk_at(6))

        @pl.when(s >= 6)
        def _():
            i = lax.div(s - 6, 2)
            count = jnp.where(i == NC - 1, NC // 2, i + 1)
            half_way = jnp.minimum(2 * lax.div(lax.div(count + 1, 2) + 1, 2), count)
            attend(i, jnp.where(odd, half_way, 0), jnp.where(odd, count, half_way))

        @pl.when(due(4, even))
        def _():
            kv_one(chunk_at(4))

        @pl.when(due(5, odd))
        def _():
            kv_two(chunk_at(5))

    for a in range(NC):
        total = jnp.sum(l[a], axis=1, keepdims=True)
        done = (acc[a] / total).astype(jnp.bfloat16)
        start = (a + NC - lead) % NC * chunk
        for h in range(heads):
            out[pl.ds(start, chunk), h * HD:(h + 1) * HD] = done[h * chunk:(h + 1) * chunk]

    for c in a_moves:
        c.wait_send()

    @pl.loop(0, units)
    def _(u):
        for name in hops:
            hop(u, name).wait_send()

    @pl.loop(0, NC)
    def _(i):
        exchange(i).wait_send()
        share(i, 0).wait_send()
        for dz in range(1, 4):
            @pl.when(z + dz <= 3)
            def _():
                onward(i, dz, 0).wait_send()
                onward(i, dz, 1).wait_send()

            @pl.when(z >= dz)
            def _():
                share(i, dz).wait_send()


def layer(text_first, *operands):
    rows, cols = operands[2].shape
    hidden = operands[0].shape[1]
    blocks, _, q_cols = operands[6].shape
    heads = q_cols // HD
    chunk = rows // NC
    any_space = pl.BlockSpec(memory_space=pl.ANY)
    vmem = pl.BlockSpec(memory_space=pltpu.VMEM)
    dma = pltpu.SemaphoreType.DMA
    return pl.pallas_call(
        functools.partial(layer_kernel, text_first),
        out_shape=jax.ShapeDtypeStruct((rows, q_cols), jnp.bfloat16),
        in_specs=[any_space] * 3 + [vmem] * 3 + [any_space] * 3,
        out_specs=vmem,
        scratch_shapes=[
            pltpu.VMEM((NK, rows, hidden // NK), jnp.bfloat16),
            pltpu.VMEM((NJ, NK, hidden // NK, cols // NJ), jnp.bfloat16),
            pltpu.VMEM((rows, cols // NJ), jnp.float32),
            pltpu.VMEM((NJ, rows, cols // NJ), jnp.bfloat16),
            pltpu.VMEM((NJ, rows, cols // NJ), jnp.bfloat16),
            pltpu.VMEM((8, NJ, rows, cols // NJ), jnp.bfloat16),
            pltpu.VMEM((blocks, cols, q_cols + 2 * HD), jnp.bfloat16),
            pltpu.VMEM((NC, heads * chunk, HD), jnp.bfloat16),
            pltpu.VMEM((NC, 16 * chunk, 2 * HD), jnp.bfloat16),
            pltpu.VMEM((2 * chunk, 4 * chunk), jnp.int32),
            pltpu.VMEM((NC, heads * chunk, 128), jnp.float32),
            pltpu.VMEM((NC, heads * chunk, 128), jnp.float32),
            pltpu.VMEM((NC, heads * chunk, HD), jnp.float32),
            dma(((NJ + 1) * NK + NJ,)),
            dma((3,)),
            dma((NJ, 16)),
            dma((NJ,)),
            dma((NC * NJ, 8)),
            dma((NC * NJ, 8)),
            dma((NC, 8)),
            dma((NC, 8)),
            dma((NC, 4)),
            dma((NC, 4)),
        ],
        compiler_params=pltpu.CompilerParams(
            collective_id=int(text_first), has_side_effects=True, vmem_limit_bytes=60 * 1024 * 1024
        ),
        name="layer_text_first" if text_first else "layer",
    )(*operands)


def local(merged_hidden, counts, owner, down_proj, text_embed, norm_gain, w_query, w_key, w_value):
    rows, cols = text_embed.shape
    shards, wcap = owner.shape
    blocks = norm_gain.shape[0] // cols
    q_cols = w_query.shape[1]
    live = jnp.arange(wcap, dtype=jnp.int32)[None, :] < counts[:, None]
    ids = jnp.arange(shards, dtype=jnp.int32)
    hits = (owner[:, :, None] == ids) & live[:, :, None]
    fullest = jnp.max(jnp.sum(hits.astype(jnp.int32), axis=(0, 1)))
    text_first = fullest * (rows // wcap) <= rows - LATE * (rows // NC)
    return lax.cond(
        text_first,
        functools.partial(layer, True),
        functools.partial(layer, False),
        merged_hidden,
        down_proj,
        text_embed,
        counts.reshape(1, -1),
        owner,
        norm_gain.reshape(1, -1),
        w_query.reshape(blocks, cols, q_cols),
        w_key.reshape(blocks, cols, HD),
        w_value.reshape(blocks, cols, HD),
    )


def solution(mesh):
    in_specs = (
        P(("ctx", "grp"), None),
        P(),
        P(),
        P(None, "tp"),
        P(("ctx", "grp"), "tp"),
        P(),
        P(None, "tp"),
        P(None, "tp"),
        P(None, "tp"),
    )
    out_specs = P(("ctx", "grp"), "tp")
    return jax.shard_map(local, mesh=mesh, in_specs=in_specs, out_specs=out_specs, check_vma=False)
```

```python
import functools
import math

import jax
import jax.numpy as jnp
from jax import lax
from jax.experimental import pallas as pl
from jax.experimental.pallas import tpu as pltpu
from jax.sharding import PartitionSpec as P

HD = 128
NC = 8
NJ = 2
NK = 4
AHEAD = 3
LATE = 3
MESH = pl.DeviceIdType.MESH
NEG = float("-inf")
LOWEST = -3e38


def layer_kernel(
    text_first, merged_in, down_in, text_in, counts_in, owner_in, gain, wq_in, wk_in, wv_in, out,
    merged, down, image_sum, packed, arrived, seq, w, q, kv, ahead_by, m, l, acc,
    in_sem, w_sem, as_sem, ar_sem, gs, gr, ks, kr, fs, fr,
):
    rows, cols = text_in.shape
    shards, wcap = owner_in.shape
    window = rows // wcap
    most = wcap // shards
    part = cols // NJ
    depth = merged.shape[2]
    pair_rows = most * window
    chunk = rows // NC
    half = chunk // 2
    heads = q.shape[1] // chunk
    units = NC * NJ
    lead = LATE if text_first else 0
    placed_rows = rows - lead * chunk

    def row_chunk(i):
        return lax.rem(i + NC - lead, NC)

    ctx = lax.axis_index("ctx")
    tp = lax.axis_index("tp")
    yh = lax.axis_index("grp")
    z, core = lax.div(ctx, 2), lax.rem(ctx, 2)
    yl, x = lax.div(tp, 4), lax.rem(tp, 4)
    rank = ctx * 2 + yh

    def at(dx, dy):
        return lax.rem(yl + dy, 2) * 4 + lax.rem(x + dx, 4)

    to_xp, to_xm, to_yp = {"tp": at(1, 0)}, {"tp": at(3, 0)}, {"tp": at(0, 1)}
    sibling = {"ctx": z * 2 + 1 - core}

    def shard_at(step):
        d = lax.rem(rank + step, shards)
        return d, {"ctx": lax.div(d, 2), "grp": lax.rem(d, 2)}

    barrier = pltpu.get_barrier_semaphore()
    partners = [to_xp, to_xm, to_yp] + [shard_at(n)[1] for n in range(1, shards)]
    for dev in partners:
        pl.semaphore_signal(barrier, inc=1, device_id=dev, device_id_type=MESH)

    def col(j):
        return pl.ds(j * part, part)

    loads = []
    for j in range(NJ):
        for k in range(NK):
            deep = pl.ds(k * depth, depth)
            stage = [
                pltpu.make_async_copy(
                    down_in.at[deep, col(j)], down.at[j, k], in_sem.at[j * NK + k]
                )
            ]
            if j == 0:
                stage.append(
                    pltpu.make_async_copy(
                        merged_in.at[:, deep], merged.at[k], in_sem.at[NJ * NK + k]
                    )
                )
            loads.append(stage)
    load_text = [
        pltpu.make_async_copy(text_in.at[:, col(j)], seq.at[0, j], in_sem.at[(NJ + 1) * NK + j])
        for j in range(NJ)
    ]
    load_w = [
        pltpu.make_async_copy(wk_in, w.at[:, :, pl.ds(0, HD)], w_sem.at[0]),
        pltpu.make_async_copy(wv_in, w.at[:, :, pl.ds(HD, HD)], w_sem.at[1]),
        pltpu.make_async_copy(wq_in, w.at[:, :, pl.ds(2 * HD, heads * HD)], w_sem.at[2]),
    ]
    loads.append([] if text_first else load_text)
    loads.append(load_w)
    if text_first:
        for c in load_text:
            c.start()
    for stage in loads[:3]:
        for c in stage:
            c.start()

    def remote(src, dst, ssem, rsem, dev):
        return pltpu.make_async_remote_copy(
            src_ref=src, dst_ref=dst, send_sem=ssem, recv_sem=rsem,
            device_id=dev, device_id_type=MESH,
        )

    def iota(shape, axis):
        return lax.broadcasted_iota(jnp.int32, shape, axis)

    shard_ids = iota((shards, wcap), 0)
    counts_col = jnp.sum(
        jnp.where(iota((shards, shards), 0) == iota((shards, shards), 1), counts_in[...], 0),
        axis=1, keepdims=True,
    )
    live = iota((shards, wcap), 1) < counts_col
    owner = owner_in[...]
    lane_win = lax.div(iota((wcap, rows), 1), window)
    spread = (lane_win == iota((wcap, rows), 0)).astype(jnp.float32)
    my_owner = jnp.sum(
        jnp.where(live & (shard_ids == rank), owner + 1, 0), axis=0, keepdims=True
    ).astype(jnp.float32)
    my_owner = jnp.broadcast_to(my_owner, (8, wcap))
    lane_owner = jnp.dot(my_owner, spread, preferred_element_type=jnp.float32)[:1].astype(jnp.int32)
    lane = iota((1, rows), 1)
    lane_slot = lax.div(lane, window * shards)
    slot_row = jnp.where(
        lane_owner > 0,
        (lane_owner - 1) * pair_rows + lane_slot * window + lax.rem(lane, window),
        -1,
    )
    arrivals = jnp.sum(
        (live & (owner == rank)).astype(jnp.int32), axis=1, keepdims=True
    )
    from_shard = lax.div(iota((shards, rows), 1), pair_rows)
    by_shard = iota((shards, rows), 0)
    before = jnp.sum(jnp.where(by_shard < from_shard, arrivals, 0), axis=0, keepdims=True)
    here = jnp.sum(jnp.where(by_shard == from_shard, arrivals, 0), axis=0, keepdims=True)
    pair_slot = lax.div(lax.rem(lane, pair_rows), window)
    dest_row = jnp.where(
        pair_slot < here, (before + pair_slot) * window + lax.rem(lane, window), -1
    )
    filled = jnp.sum(arrivals, axis=0, keepdims=True) * window
    row_ids = iota((rows, rows), 0)
    select = (row_ids == slot_row).astype(jnp.float32).astype(jnp.bfloat16)
    place = (row_ids == dest_row).astype(jnp.float32).astype(jnp.bfloat16)[:placed_rows]
    is_image = iota((placed_rows, part), 0) < filled

    key = iota(ahead_by.shape, 1)
    dc, dy = lax.div(key, 2 * chunk), lax.rem(lax.div(key, chunk), 2)
    peer = jnp.where(dc == 0, core, 1 - core) * 2 + jnp.where(dy == 0, yh, 1 - yh)
    ahead_by[...] = (
        (peer - core * 2 - yh) * rows + lax.rem(key, chunk)
        - lax.rem(iota(ahead_by.shape, 0), chunk)
    )
    m[...] = jnp.full(m.shape, LOWEST, jnp.float32)
    l[...] = jnp.zeros(l.shape, jnp.float32)
    acc[...] = jnp.zeros(acc.shape, jnp.float32)

    def project_image(j):
        for k in range(NK):
            for c in loads[j * NK + k]:
                c.wait()
            if j * NK + k + 3 < len(loads):
                for c in loads[j * NK + k + 3]:
                    c.start()
            term = jnp.dot(merged[k], down[j, k], preferred_element_type=jnp.float32)
            if k == 0:
                image_sum[...] = term
            elif k < NK - 1:
                image_sum[...] += term
        image = (image_sum[...] + term).astype(jnp.bfloat16)
        packed[j] = jnp.dot(select, image, preferred_element_type=jnp.float32).astype(
            jnp.bfloat16
        )

    def own_pair():
        return pl.ds(pl.multiple_of(rank * pair_rows, pair_rows), pair_rows)

    a_moves = []

    def send_windows(j):
        for n in range(1, shards):
            d, dev = shard_at(n)
            there = pl.ds(pl.multiple_of(d * pair_rows, pair_rows), pair_rows)
            c = remote(
                packed.at[j, there], arrived.at[j, own_pair()], as_sem.at[j, n], ar_sem.at[j], dev
            )
            c.start()
            a_moves.append(c)
        arrived[j, own_pair(), :] = packed[j, own_pair(), :]

    def place_windows(j):
        others = pl.ds(0, (shards - 1) * pair_rows)
        remote(
            packed.at[j, others], arrived.at[j, others], as_sem.at[j, 0], ar_sem.at[j], sibling
        ).wait_recv()
        if not text_first:
            load_text[j].wait()
        placed = jnp.dot(place, arrived[j], preferred_element_type=jnp.float32)
        text = seq[0, j, :placed_rows].astype(jnp.float32)
        seq[0, j, :placed_rows] = jnp.where(is_image, placed, text).astype(jnp.bfloat16)

    hops = {
        "own_y": (0, 3, 0, chunk, to_yp, 0),
        "own_xp": (0, 1, 0, chunk, to_xp, 1),
        "own_xm": (0, 2, 0, chunk, to_xm, 2),
        "opp_a": (1, 6, 0, half, to_xp, 3),
        "opp_b": (2, 6, half, half, to_xm, 4),
        "mate_xp": (3, 4, 0, chunk, to_xp, 5),
        "mate_xm": (3, 5, 0, chunk, to_xm, 6),
        "opp_y": (6, 7, 0, chunk, to_yp, 7),
        "less_xp": (3, 4, 0, chunk - 16, to_xp, 5),
        "less_xm": (3, 5, 0, chunk - 16, to_xm, 6),
        "side_a": (1, 4, chunk - 16, 16, to_yp, 8),
        "side_b": (2, 5, chunk - 16, 16, to_yp, 9),
    }
    even_hops = [n for n in hops if n not in ("less_xp", "less_xm", "side_a", "side_b")]
    odd_hops = [n for n in hops if n not in ("mate_xp", "mate_xm")]

    def is_odd(u):
        return lax.rem(u, 2) == 1

    def hop(u, name):
        src, dst, start, size, dev, index = hops[name]
        i, j = lax.div(u, NJ), lax.rem(u, NJ)
        r = pl.ds(pl.multiple_of(row_chunk(i) * chunk + start, 16), size)
        return remote(
            seq.at[src, j, r], seq.at[dst, j, r], gs.at[u, index], gr.at[u, index], dev
        )

    def first(u):
        hop(u, "own_y").start()
        hop(u, "own_xp").start()
        hop(u, "own_xm").start()

    def second(u):
        hop(u, "own_xp").wait_recv()
        hop(u, "opp_a").start()
        hop(u, "own_xm").wait_recv()
        hop(u, "opp_b").start()
        hop(u, "own_y").wait_recv()

        @pl.when(is_odd(u))
        def _():
            hop(u, "less_xp").start()
            hop(u, "less_xm").start()
            hop(u, "side_a").start()
            hop(u, "side_b").start()

        @pl.when(jnp.logical_not(is_odd(u)))
        def _():
            hop(u, "mate_xp").start()
            hop(u, "mate_xm").start()

    def third(u):
        hop(u, "opp_a").wait_recv()
        hop(u, "opp_b").wait_recv()
        hop(u, "opp_y").start()

    places = [(0, 0), (3, 0), (1, 0), (0, 1), (3, 1), (1, 1), (2, 0), (2, 1)]

    def cut(dz, dc, dy, size):
        return pl.ds(((dz * 2 + dc) * 2 + dy) * chunk, size)

    def to_z(dz):
        return {"ctx": lax.rem(z + dz, 4) * 2 + core}

    def exchange(i):
        return remote(
            kv.at[i, cut(0, 0, 0, chunk)], kv.at[i, cut(0, 0, 1, chunk)],
            ks.at[i, 0], kr.at[i, 0], {"grp": 1 - yh},
        )

    def onward(i, dz, dy):
        index = 4 * dy + dz
        return remote(
            kv.at[i, cut(0, 0, dy, chunk)], kv.at[i, cut(dz, 0, dy, chunk)],
            ks.at[i, index], kr.at[i, index], to_z(dz),
        )

    def share(i, dz):
        return remote(
            kv.at[i, cut(dz, 0, 0, 2 * chunk)], kv.at[i, cut(dz, 1, 0, 2 * chunk)],
            fs.at[i, dz], fr.at[i, dz], sibling,
        )

    def project(i):
        r = pl.ds(pl.multiple_of(row_chunk(i) * chunk, chunk), chunk)
        for j in range(NJ):
            names = ("less_xp", "less_xm", "side_a", "side_b") if j else ("mate_xp", "mate_xm")
            for name in names + ("opp_y",):
                hop(i * NJ + j, name).wait_recv()

        def block(k):
            return jnp.concatenate([seq[k, j, r] for j in range(NJ)], axis=1).astype(jnp.float32)

        total = jnp.zeros((chunk, 128), jnp.float32)
        for k in range(8):
            v = block(k)
            squares = v * v
            for c in range(cols // 128):
                total = total + squares[:, c * 128:(c + 1) * 128]
        scale = lax.rsqrt(jnp.sum(total, axis=1, keepdims=True) / (8 * cols) + 1e-06)
        result = None
        for k in range(8):
            b = at(*places[k])
            g = gain[:, pl.ds(pl.multiple_of(b * cols, cols), cols)]
            normed = (block(k) * scale * g).astype(jnp.bfloat16)
            term = jnp.dot(normed, w[b], preferred_element_type=jnp.float32)
            result = term if result is None else result + term
        kv[i, cut(0, 0, 0, chunk)] = result[:, :2 * HD].astype(jnp.bfloat16)
        exchange(i).start()
        for dz in range(1, 4):
            @pl.when(z + dz <= 3)
            def _():
                onward(i, dz, 0).start()
        for h in range(heads):
            q[i, h * chunk:(h + 1) * chunk] = result[
                :, (h + 2) * HD:(h + 3) * HD
            ].astype(jnp.bfloat16)

    def kv_one(i):
        exchange(i).wait_recv()
        for dz in range(1, 4):
            @pl.when(z + dz <= 3)
            def _():
                onward(i, dz, 1).start()
        share(i, 0).start()

    def kv_two(i):
        for dz in range(1, 4):
            @pl.when(z >= dz)
            def _():
                onward(i, dz, 0).wait_recv()
                onward(i, dz, 1).wait_recv()
                share(i, dz).start()

    def kv_three(i):
        share(i, 0).wait_recv()
        for dz in range(1, 4):
            @pl.when(z >= dz)
            def _():
                share(i, dz).wait_recv()

    scale2 = math.log2(math.e) / math.sqrt(HD)
    tile = 2 * chunk

    def attend_tiles(pairs, keys):
        work = [(a, pl.ds(t * tile, tile), b) for a, b in pairs for t in range(q.shape[1] // tile)]

        def score(n):
            a, r, b = work[n]
            return lax.dot_general(
                q[a, r], kv[b, :keys, :HD], (((1,), (1,)), ((), ())),
                preferred_element_type=jnp.float32,
            )

        def finish(a, r, b, fade, probs):
            acc[a, r] = acc[a, r] * fade + jnp.dot(
                probs, kv[b, :keys, HD:], preferred_element_type=jnp.float32
            )

        coming = score(0)
        pending = None
        for n, (a, r, b) in enumerate(work):
            s = coming
            if n + 1 < len(work):
                coming = score(n + 1)
            cuts = [s[:, c * 128:(c + 1) * 128] for c in range(keys // 128)]
            for c in range(4 * chunk // 128):
                seen = ahead_by[:, c * 128:(c + 1) * 128] <= (row_chunk(a) - row_chunk(b)) * chunk
                cuts[c] = jnp.where(seen, cuts[c], NEG)
            top = jnp.max(functools.reduce(jnp.maximum, cuts), axis=1, keepdims=True)
            old = m[a, r]
            new = jnp.maximum(old, top)
            m[a, r] = new
            fade = jnp.exp2((old - new) * scale2)
            probs = [jnp.exp2((c - new) * scale2) for c in cuts]
            l[a, r] = l[a, r] * fade + functools.reduce(jnp.add, probs)
            probs = jnp.concatenate([p.astype(jnp.bfloat16) for p in probs], axis=1)
            if pending is not None:
                finish(*pending)
            pending = (a, r, b, fade, probs)
        finish(*pending)

    def attend(i, low, high):
        seen = jnp.minimum(i + 2, NC)

        def pair_of(n):
            column = n < seen
            return jnp.where(column, n, jnp.minimum(i + 1, NC - 1)), jnp.where(column, i, n - seen)

        fours = lax.div(high - low, 2)
        for level in range(4):
            keys = (level + 1) * 4 * chunk

            @pl.when(z == level)
            def _():
                @pl.loop(0, fours)
                def _(t):
                    at_pair = 2 * (low + 2 * t)
                    attend_tiles([pair_of(at_pair + n) for n in range(4)], keys)

                @pl.when(high - low > 2 * fours)
                def _():
                    attend_tiles([pair_of(2 * high - 2), pair_of(2 * high - 1)], keys)

    def forwards(s):
        @pl.when(s <= units)
        def _():
            third(s - 1)

        @pl.when(jnp.logical_and(s >= 4, s < units))
        def _():
            second(s)

        @pl.when(s + AHEAD < units)
        def _():
            first(s + AHEAD)

    if text_first:
        for c in load_text:
            c.wait()
        pl.semaphore_wait(barrier, len(partners))
        for u in range(LATE * NJ):
            first(u)
        project_image(0)
        send_windows(0)
        second(0)
        second(1)
        project_image(1)
        send_windows(1)
        third(0)
        third(1)
        second(2)
        second(3)
        for c in load_w:
            c.wait()
        place_windows(0)
        place_windows(1)
    else:
        for j in range(NJ):
            project_image(j)
            if j == 0:
                pl.semaphore_wait(barrier, len(partners))
            send_windows(j)
        early = [u for u in range(AHEAD + 2) if u % NJ == 0]
        late = [u for u in range(AHEAD + 2) if u % NJ]
        place_windows(0)
        for u in early:
            first(u)
        second(0)
        place_windows(1)
        for u in late:
            first(u)
        for c in load_w:
            c.wait()
        third(0)
        second(1)
        third(1)
        second(2)
        first(AHEAD + 2)
        second(3)

    @pl.loop(3, 2 * NC + 6)
    def _(s):
        forwards(s)
        odd = lax.rem(s, 2) == 1
        even = jnp.logical_not(odd)

        def chunk_at(lag):
            return lax.div(s - lag, 2)

        def due(lag, parity):
            return jnp.logical_and(
                parity, jnp.logical_and(s >= lag, s - lag <= 2 * (NC - 1))
            )

        @pl.when(due(3, odd))
        def _():
            project(chunk_at(3))

        @pl.when(due(6, even))
        def _():
            kv_three(chunk_at(6))

        @pl.when(s >= 6)
        def _():
            i = lax.div(s - 6, 2)
            count = jnp.where(i == NC - 1, NC // 2, i + 1)
            half_way = jnp.minimum(2 * lax.div(lax.div(count + 1, 2) + 1, 2), count)
            attend(i, jnp.where(odd, half_way, 0), jnp.where(odd, count, half_way))

        @pl.when(due(4, even))
        def _():
            kv_one(chunk_at(4))

        @pl.when(due(5, odd))
        def _():
            kv_two(chunk_at(5))

    for a in range(NC):
        total = jnp.sum(l[a], axis=1, keepdims=True)
        done = (acc[a] / total).astype(jnp.bfloat16)
        start = (a + NC - lead) % NC * chunk
        for h in range(heads):
            out[pl.ds(start, chunk), h * HD:(h + 1) * HD] = done[h * chunk:(h + 1) * chunk]

    for c in a_moves:
        c.wait_send()

    @pl.loop(0, units)
    def _(u):
        @pl.when(is_odd(u))
        def _():
            for name in odd_hops:
                hop(u, name).wait_send()

        @pl.when(jnp.logical_not(is_odd(u)))
        def _():
            for name in even_hops:
                hop(u, name).wait_send()

    @pl.loop(0, NC)
    def _(i):
        exchange(i).wait_send()
        share(i, 0).wait_send()
        for dz in range(1, 4):
            @pl.when(z + dz <= 3)
            def _():
                onward(i, dz, 0).wait_send()
                onward(i, dz, 1).wait_send()

            @pl.when(z >= dz)
            def _():
                share(i, dz).wait_send()


def layer(text_first, *operands):
    rows, cols = operands[2].shape
    hidden = operands[0].shape[1]
    blocks, _, q_cols = operands[6].shape
    heads = q_cols // HD
    chunk = rows // NC
    any_space = pl.BlockSpec(memory_space=pl.ANY)
    vmem = pl.BlockSpec(memory_space=pltpu.VMEM)
    dma = pltpu.SemaphoreType.DMA
    return pl.pallas_call(
        functools.partial(layer_kernel, text_first),
        out_shape=jax.ShapeDtypeStruct((rows, q_cols), jnp.bfloat16),
        in_specs=[any_space] * 3 + [vmem] * 3 + [any_space] * 3,
        out_specs=vmem,
        scratch_shapes=[
            pltpu.VMEM((NK, rows, hidden // NK), jnp.bfloat16),
            pltpu.VMEM((NJ, NK, hidden // NK, cols // NJ), jnp.bfloat16),
            pltpu.VMEM((rows, cols // NJ), jnp.float32),
            pltpu.VMEM((NJ, rows, cols // NJ), jnp.bfloat16),
            pltpu.VMEM((NJ, rows, cols // NJ), jnp.bfloat16),
            pltpu.VMEM((8, NJ, rows, cols // NJ), jnp.bfloat16),
            pltpu.VMEM((blocks, cols, q_cols + 2 * HD), jnp.bfloat16),
            pltpu.VMEM((NC, heads * chunk, HD), jnp.bfloat16),
            pltpu.VMEM((NC, 16 * chunk, 2 * HD), jnp.bfloat16),
            pltpu.VMEM((2 * chunk, 4 * chunk), jnp.int32),
            pltpu.VMEM((NC, heads * chunk, 128), jnp.float32),
            pltpu.VMEM((NC, heads * chunk, 128), jnp.float32),
            pltpu.VMEM((NC, heads * chunk, HD), jnp.float32),
            dma(((NJ + 1) * NK + NJ,)),
            dma((3,)),
            dma((NJ, 16)),
            dma((NJ,)),
            dma((NC * NJ, 10)),
            dma((NC * NJ, 10)),
            dma((NC, 8)),
            dma((NC, 8)),
            dma((NC, 4)),
            dma((NC, 4)),
        ],
        compiler_params=pltpu.CompilerParams(
            collective_id=int(text_first), has_side_effects=True, vmem_limit_bytes=60 * 1024 * 1024
        ),
        name="layer_text_first" if text_first else "layer",
    )(*operands)


def local(merged_hidden, counts, owner, down_proj, text_embed, norm_gain, w_query, w_key, w_value):
    rows, cols = text_embed.shape
    shards, wcap = owner.shape
    blocks = norm_gain.shape[0] // cols
    q_cols = w_query.shape[1]
    live = jnp.arange(wcap, dtype=jnp.int32)[None, :] < counts[:, None]
    ids = jnp.arange(shards, dtype=jnp.int32)
    hits = (owner[:, :, None] == ids) & live[:, :, None]
    fullest = jnp.max(jnp.sum(hits.astype(jnp.int32), axis=(0, 1)))
    text_first = fullest * (rows // wcap) <= rows - LATE * (rows // NC)
    return lax.cond(
        text_first,
        functools.partial(layer, True),
        functools.partial(layer, False),
        merged_hidden,
        down_proj,
        text_embed,
        counts.reshape(1, -1),
        owner,
        norm_gain.reshape(1, -1),
        w_query.reshape(blocks, cols, q_cols),
        w_key.reshape(blocks, cols, HD),
        w_value.reshape(blocks, cols, HD),
    )


def solution(mesh):
    in_specs = (
        P(("ctx", "grp"), None),
        P(),
        P(),
        P(None, "tp"),
        P(("ctx", "grp"), "tp"),
        P(),
        P(None, "tp"),
        P(None, "tp"),
        P(None, "tp"),
    )
    out_specs = P(("ctx", "grp"), "tp")
    return jax.shard_map(local, mesh=mesh, in_specs=in_specs, out_specs=out_specs, check_vma=False)
```
